32 devices in a mesh: groups: 2 (over y), az: 4 (over z), rad: 4 (over x, core).
Axes of the slice: x: 2, y: 2, z: 4, core: 2. Of those that a mesh axis runs over, the one named last changes fastest.
Arguments:
- density: float32 [256, 1024], P(('groups', 'rad'), 'az'), parts along dimension 0, may hold values from 0.5 to 1.5
- momentum: float32 [4, 128, 1024], P('groups', 'rad', 'az'), parts along dimension 0, may hold values from -1 to 1
- shear_shift: int32 [4], P('groups'), parts along dimension 0, may hold values from 0 to 1023
- shear_frac: float32 [4], P('groups'), parts along dimension 0, may hold values from 0 to 1
- advect_shift: int32 [256], P(('groups', 'rad')), parts along dimension 0, may hold values from 0 to 1023
- advect_frac: float32 [256], P(('groups', 'rad')), parts along dimension 0, may hold values from 0 to 1
- rotation: float32 [2], P('groups'), parts along dimension 0, may hold values from 0.5 to 2
Outputs:
- density_out: float32 [256, 1024], P(('groups', 'rad'), 'az'), parts along dimension 0
- momentum_out: float32 [4, 128, 1024], P('groups', 'rad', 'az'), parts along dimension 0
The draws below stay inside these ranges and needn't reach their ends.
There are 2 independent parts, one for each index of `groups`. The reference program is written for one: setup_inputs(seed, part) draws one part's arguments, and reference() takes and returns one part's arrays. A program takes and returns all parts, laid end to end along the dimension named above; each array names one. Nothing has to cross between parts.
All inputs are finite; a program needn't handle non-finite values.
Results may differ from the reference program's by a relative error of at most 0.0003.
Values sent between devices are 32-bit elements; how exact they have to be, the bound alone decides.
No kernel may reach another device: no remote copies, remote signals or barrier semaphores. Data moves between devices by JAX's collectives and lax.ppermute only.
A program may use at most 64 MiB of HBM per device.

```python
import math
import jax
import jax.numpy as jnp
from jax import lax

NX = 128
NY = 1024


def touch_ends(result, stream_key, least, largest):
    longest = result.shape.index(max(result.shape))
    spots = []
    for shift in (0, 1):
        where = [jax.random.randint(jax.random.fold_in(stream_key, axis), (), 0, length) for axis, length in enumerate(result.shape)]
        where[longest] = (where[longest] + shift) % result.shape[longest]
        spots.append(tuple(where))
    return result.at[spots[0]].set(least).at[spots[1]].set(largest)


def levels(rng, shape, split, smallest, largest):
    def one(dim, shards_of):
        draws = jax.random.uniform(jax.random.fold_in(jax.random.fold_in(rng, 6), dim), (shards_of,), jnp.float32, smallest / len(split), largest / len(split))
        return jnp.repeat(jnp.exp(draws), shape[dim] // shards_of).reshape((-1,) + (1,) * (len(shape) - dim - 1))

    factor_of = one(*split[0])
    for cut in split[1:]:
        factor_of = factor_of * one(*cut)
    return factor_of


def centred(own_key, shape, deviation, bound, shards=(), held_as=jnp.bfloat16):
    values = jax.random.normal(own_key, shape, jnp.float32) * deviation
    if len(shards) > 0:
        values = levels(own_key, shape, shards, -0.22, 0.18) * values
    return jnp.clip(values, min=-bound, max=bound).astype(held_as)


def setup_inputs(seed: int = 0, part: int = 0) -> dict:
    key_of = jax.random.split(jax.random.key(seed), 8)
    own_keys = jax.random.split(jax.random.fold_in(key_of[7], part), 8)
    density = jnp.clip(0.5 + 1.0 * jax.random.uniform(own_keys[0], (NX, NY), jnp.float32) ** levels(own_keys[0], (NX, NY), ((0, 4), (1, 4)), -0.2, 0.2), 0.5, 1.5)
    momentum = centred(own_keys[1], (2, NX, NY), 0.25, 1.0, ((1, 4), (2, 4)), jnp.float32)
    shear_shift = jax.random.randint(own_keys[2], (2,), 0, NY).astype(jnp.int32)
    shear_frac = jnp.clip(jax.random.uniform(own_keys[3], (2,), jnp.float32, 0.0, 1.0), 0.0, 1.0)
    advect_shift = touch_ends(jax.random.randint(own_keys[4], (NX,), 0, NY), jax.random.fold_in(own_keys[4], 1), 0, NY - 1).astype(jnp.int32)
    advect_frac = jnp.clip(1.0 * jax.random.uniform(own_keys[5], (NX,), jnp.float32) ** levels(own_keys[5], (NX,), ((0, 4),), -0.2, 0.2), 0.0, 1.0)
    rotation = jnp.clip(jnp.exp(jax.random.uniform(own_keys[6], (1,), jnp.float32, math.log(0.5), math.log(2.0))), 0.5, 2.0)
    return {"density": density, "momentum": momentum, "shear_shift": shear_shift, "shear_frac": shear_frac, "advect_shift": advect_shift, "advect_frac": advect_frac, "rotation": rotation}


time_step = 0.12
sound_speed = 1.0


def minmod(first, second):
    return 0.5 * (jnp.sign(first) + jnp.sign(second)) * jnp.minimum(jnp.abs(first), jnp.abs(second))


def trimmed(array, lower, upper, direction):
    return lax.slice_in_dim(array, lower, array.shape[direction] - upper, axis=direction)


def physical(state):
    mass_flux = state[0] * state[1]
    fluxes = jnp.stack([mass_flux, mass_flux * state[1] + sound_speed * sound_speed * state[0], mass_flux * state[2]])
    conserved = jnp.stack([state[0], state[0] * state[1], state[0] * state[2]])
    return fluxes, conserved


def face_flux(left_state, right_state):
    left_flux, left_cons = physical(left_state)
    right_flux, right_cons = physical(right_state)
    signal = jnp.maximum(jnp.abs(left_state[1]), jnp.abs(right_state[1])) + sound_speed
    return 0.5 * (left_flux + right_flux) - 0.5 * signal * (right_cons - left_cons)


def primitive(conserved, normal):
    return jnp.stack([conserved[0], conserved[normal] / conserved[0], conserved[3 - normal] / conserved[0]])


def sweep_axis(prims, direction):
    slopes = minmod(trimmed(prims, 1, 1, direction) - trimmed(prims, 0, 2, direction),
                    trimmed(prims, 2, 0, direction) - trimmed(prims, 1, 1, direction))
    left_state = trimmed(prims, 1, 2, direction) + 0.5 * trimmed(slopes, 0, 1, direction)
    right_state = trimmed(prims, 2, 1, direction) - 0.5 * trimmed(slopes, 1, 0, direction)
    fluxes = face_flux(left_state, right_state)
    return trimmed(fluxes, 1, 0, direction) - trimmed(fluxes, 0, 1, direction)


def rolled(rows, offset_cells):
    cells = jnp.arange(NY, dtype=jnp.int32)
    index = (cells - offset_cells) % NY
    return jnp.take(rows, index, axis=2)


def tendency(state, offset_cells, fraction, rotation):
    below = state[:, -2:]
    above = state[:, :2]
    lower_ghost = (1.0 - fraction) * rolled(below, offset_cells) + fraction * rolled(below, offset_cells + 1)
    upper_ghost = (1.0 - fraction) * rolled(above, -offset_cells) + fraction * rolled(above, -offset_cells - 1)
    columns = jnp.concatenate([lower_ghost, state, upper_ghost], axis=1)
    cycle_rows = jnp.concatenate([state[:, :, -2:], state, state[:, :, :2]], axis=2)
    radial_div = sweep_axis(primitive(columns, 1), 1)
    azimuth_div = sweep_axis(primitive(cycle_rows, 2), 2)
    azimuth_div = jnp.stack([azimuth_div[0], azimuth_div[2], azimuth_div[1]])
    source = jnp.stack([jnp.zeros_like(state[0]), 2.0 * rotation * state[2], -0.5 * rotation * state[1]])
    return -(radial_div + azimuth_div) + source


def reference(density, momentum, shear_shift, shear_frac, advect_shift, advect_frac, rotation):
    state = jnp.concatenate([density[None], momentum], axis=0)
    middle = state + time_step * tendency(state, shear_shift[0], shear_frac[0], rotation[0])
    final = 0.5 * state + 0.5 * (middle + time_step * tendency(middle, shear_shift[1], shear_frac[1], rotation[0]))
    cells = jnp.arange(NY, dtype=jnp.int32)
    first_index = (cells[None, :] - advect_shift[:, None].astype(jnp.int32)) % NY
    second_index = (first_index - 1) % NY
    weight = advect_frac[None, :, None]
    remapped = (1.0 - weight) * jnp.take_along_axis(final, jnp.broadcast_to(first_index[None], final.shape), axis=2) \
        + weight * jnp.take_along_axis(final, jnp.broadcast_to(second_index[None], final.shape), axis=2)
    return remapped[0], remapped[1:]
```

```python
import functools

import jax
import jax.numpy as jnp
from jax import lax
from jax.experimental import pallas as pl
from jax.experimental.pallas import tpu as pltpu
from jax.sharding import PartitionSpec as P

TIME_STEP = 0.12
SOUND_SPEED = 1.0
LANES = 128
HALO = 4
UNROLL = 8


def turned(value, whole, part, lane):
    lanes = pltpu.roll(value, part, 1)
    same = pltpu.roll(lanes, whole, 0)
    before = pltpu.roll(same, 1, 0)
    return jnp.where(lane < part, before, same)


def previous(value, lane):
    lanes = pltpu.roll(value, 1, 1)
    return jnp.where(lane == 0, pltpu.roll(lanes, 1, 0), lanes)


def following(value, lane):
    lanes = pltpu.roll(value, LANES - 1, 1)
    return jnp.where(lane == LANES - 1, pltpu.roll(lanes, value.shape[0] - 1, 0), lanes)


def minmod(first, second):
    return jnp.maximum(jnp.minimum(second, 0.0), jnp.minimum(first, jnp.maximum(second, 0.0)))


def sums(left, right):
    signal = jnp.maximum(jnp.abs(left[1]), jnp.abs(right[1])) + 1.0
    lower = left[0] * (left[1] + signal)
    upper = right[0] * (right[1] - signal)
    return (
        lower + upper,
        (left[1] * lower + left[0]) + (right[1] * upper + right[0]),
        left[2] * lower + right[2] * upper,
    )


def minus(first, second):
    return tuple(a - b for a, b in zip(first, second))


def plus(first, second):
    return tuple(a + b for a, b in zip(first, second))


def primitives(state):
    inverse = 1.0 / state[0]
    whole = (state[0], state[1] * inverse, state[2] * inverse)
    return whole, tuple(0.5 * w for w in whole)


def azimuthal(whole, half, lane):
    normal = (whole[0], whole[2], whole[1])
    halves = (half[0], half[2], half[1])
    ahead = minus(tuple(following(h, lane) for h in halves), halves)
    behind = tuple(previous(a, lane) for a in ahead)
    slope = tuple(minmod(b, a) for b, a in zip(behind, ahead))
    left = plus(normal, slope)
    right = tuple(following(r, lane) for r in minus(normal, slope))
    face = sums(left, right)
    out = minus(face, tuple(previous(f, lane) for f in face))
    return out[0], out[2], out[1]


def sweep(load, emit, count, lane, unroll):
    def advance(row, carry):
        state = load(row)
        whole, half = primitives(state)
        ahead = minus(half, carry["half"])
        slope = tuple(minmod(b, a) for b, a in zip(carry["ahead"], ahead))
        right = minus(carry["whole"], slope)
        left = plus(carry["whole"], slope)
        face = sums(carry["left"], right)
        new = {
            "half": half,
            "whole": whole,
            "ahead": ahead,
            "left": left,
            "face": face,
            "turn": azimuthal(carry["whole"], carry["half"], lane),
        }
        return new, minus(face, carry["face"])

    def opened(row):
        first, second, third, fourth = (primitives(load(row + k)) for k in range(4))
        ahead = [minus(second[1], first[1]), minus(third[1], second[1]), minus(fourth[1], third[1])]
        slopes = [
            tuple(minmod(b, a) for b, a in zip(ahead[k], ahead[k + 1])) for k in range(2)
        ]
        return {
            "half": fourth[1],
            "whole": fourth[0],
            "ahead": ahead[2],
            "left": plus(third[0], slopes[1]),
            "face": sums(plus(second[0], slopes[0]), minus(third[0], slopes[1])),
            "turn": azimuthal(third[0], third[1], lane),
        }

    def body(block, carry):
        for step in range(unroll):
            row = block * unroll + step
            new, across = advance(row + 4, carry)
            emit(row + 2, tuple(a + b for a, b in zip(across, carry["turn"])))
            carry = new
        return carry

    opening = opened(0)
    if count == unroll:
        body(0, opening)
    else:
        lax.fori_loop(0, count // unroll, body, opening)


def step_kernel(sizes, *refs):
    tiles, radials, rows, columns, sub = sizes
    per_tile = columns // LANES
    shear_shift, shear_frac, advect_shift, advect_frac, rotation, density, momentum = refs[:7]
    pieces = refs[7 : 7 + 2 * (tiles - 1)]
    low, high, density_out, momentum_out, start, middle, remapped = refs[7 + 2 * (tiles - 1) :]
    lane = lax.broadcasted_iota(jnp.int32, (sub, LANES), 1)
    az = lax.axis_index("az")
    radial = lax.axis_index("rad")
    unroll = UNROLL
    main = 6
    end = main + rows + 4

    def place(value, component, row, tile, part):
        first = row * sub + tile * per_tile + part
        start[component, pl.ds(first, value.shape[0], stride=sub), :] = value

    for away in range(tiles):
        tile = az ^ away
        dens, mom = (density, momentum) if away == 0 else pieces[2 * away - 2 : 2 * away]
        for part in range(per_tile):
            cut = slice(part * LANES, (part + 1) * LANES)
            for row in range(0, rows, 8):
                place(dens[row : row + 8, cut], 0, main + 2 + row, tile, part)
                for way in range(2):
                    place(mom[way, row : row + 8, cut], 1 + way, main + 2 + row, tile, part)
            for component in range(3):
                place(low[component, HALO * away : HALO * away + HALO, cut], component, 0, tile, part)
                place(high[component, HALO * away : HALO * away + HALO, cut], component, end + 2, tile, part)

    def row_of(ref, component, row):
        return ref[component, pl.ds(pl.multiple_of(row * sub, 8), sub), :]

    def state_of(ref, row):
        return tuple(row_of(ref, component, row) for component in range(3))

    def put(ref, row, state):
        for component in range(3):
            ref[component, pl.ds(pl.multiple_of(row * sub, 8), sub), :] = state[component]

    at_low = radial == 0
    at_high = radial == radials - 1
    total = sub * LANES

    def from_below(state, section, here):
        shift = jnp.where(here, shear_shift[section], 0)
        weight = jnp.where(here, shear_frac[section], 0.0)
        moved = tuple(turned(s, shift // LANES, shift % LANES, lane) for s in state)
        return tuple((1.0 - weight) * m + weight * previous(m, lane) for m in moved)

    def from_above(state, section, here):
        shift = jnp.where(here, (total - shear_shift[section]) % total, 0)
        weight = jnp.where(here, shear_frac[section], 0.0)
        moved = tuple(turned(s, shift // LANES, shift % LANES, lane) for s in state)
        return tuple((1.0 - weight) * m + weight * following(m, lane) for m in moved)

    for k in range(2):
        put(start, main + k, from_below(state_of(start, 2 + k), 0, at_low))
        put(start, end - 2 + k, from_above(state_of(start, end + 2 + k), 0, at_high))
        put(start, 4 + k, from_above(state_of(start, main + 2 + k), 0, at_low))
        put(start, end + k, from_below(state_of(start, end - 4 + k), 0, at_high))

    spin = rotation[0]

    def changed(state, double):
        half_step = 0.5 * TIME_STEP
        return (
            state[0] - half_step * double[0],
            state[1] - half_step * double[1] + (2.0 * TIME_STEP) * spin * state[2],
            state[2] - half_step * double[2] - (0.5 * TIME_STEP) * spin * state[1],
        )

    def emit_first(offset, target):
        def emit(row, double):
            put(middle, row + target, changed(state_of(start, row + offset), double))
        return emit

    sweep(lambda row: state_of(start, row + main), emit_first(main, 0), rows, lane, unroll)

    def edge(which, carry):
        offset = which * end
        target = which * (rows + 2) - 2
        sweep(lambda row: state_of(start, row + offset), emit_first(offset, target), 2, lane, 2)
        return carry

    lax.fori_loop(0, 2, edge, 0)
    for k in range(2):
        put(middle, k, from_below(state_of(middle, k), 1, at_low))
        put(middle, rows + 2 + k, from_above(state_of(middle, rows + 2 + k), 1, at_high))

    def emit_second(row, double):
        new = changed(state_of(middle, row), double)
        old = state_of(start, row + main)
        final = tuple(0.5 * o + 0.5 * n for o, n in zip(old, new))
        shift = advect_shift[row - 2]
        weight = advect_frac[row - 2]
        moved = tuple(turned(f, shift // LANES, shift % LANES, lane) for f in final)
        put(remapped, row - 2, tuple((1.0 - weight) * m + weight * previous(m, lane) for m in moved))

    sweep(lambda row: state_of(middle, row), emit_second, rows, lane, unroll)

    for part in range(per_tile):
        cut = slice(part * LANES, (part + 1) * LANES)
        for row in range(0, rows, 8):
            first = row * sub + az * per_tile + part
            for component in range(3):
                value = remapped[component, pl.ds(first, 8, stride=sub), :]
                if component == 0:
                    density_out[row : row + 8, cut] = value
                else:
                    momentum_out[component - 1, row : row + 8, cut] = value


def passed_along(value, axis, steps):
    count = lax.axis_size(axis)
    pairs = [(source, (source + steps) % count) for source in range(count)]
    return lax.ppermute(value, axis, pairs)


def padded_2(block, sides, width):
    for axis, dim in sides:
        count = lax.axis_size(axis)
        forward = [(i, i + 1) for i in range(count - 1)]
        forward.append((count - 1, 0))
        backward = [(target, source) for source, target in forward]
        low = lax.ppermute(
            lax.slice_in_dim(block, block.shape[dim] - width, None, axis=dim), axis, forward
        )
        high = lax.ppermute(lax.slice_in_dim(block, 0, width, axis=dim), axis, backward)
        block = jnp.concatenate([low, block, high], axis=dim)
    return block


def signed_minmod(first, second):
    return 0.5 * (jnp.sign(first) + jnp.sign(second)) * jnp.minimum(jnp.abs(first), jnp.abs(second))


def trimmed(array, lower, upper, direction):
    return lax.slice_in_dim(array, lower, array.shape[direction] - upper, axis=direction)


def physical(state):
    mass_flux = state[0] * state[1]
    fluxes = jnp.stack(
        [
            mass_flux,
            mass_flux * state[1] + SOUND_SPEED * SOUND_SPEED * state[0],
            mass_flux * state[2],
        ]
    )
    conserved = jnp.stack([state[0], state[0] * state[1], state[0] * state[2]])
    return (fluxes, conserved)


def face_flux(left_state, right_state):
    left_flux, left_cons = physical(left_state)
    right_flux, right_cons = physical(right_state)
    signal = jnp.maximum(jnp.abs(left_state[1]), jnp.abs(right_state[1])) + SOUND_SPEED
    return 0.5 * (left_flux + right_flux) - 0.5 * signal * (right_cons - left_cons)


def primitive(conserved, normal):
    return jnp.stack(
        [conserved[0], conserved[normal] / conserved[0], conserved[3 - normal] / conserved[0]]
    )


def sweep_axis(prims, direction):
    slopes = signed_minmod(
        trimmed(prims, 1, 1, direction) - trimmed(prims, 0, 2, direction),
        trimmed(prims, 2, 0, direction) - trimmed(prims, 1, 1, direction),
    )
    left_state = trimmed(prims, 1, 2, direction) + 0.5 * trimmed(slopes, 0, 1, direction)
    right_state = trimmed(prims, 2, 1, direction) - 0.5 * trimmed(slopes, 1, 0, direction)
    fluxes = face_flux(left_state, right_state)
    return trimmed(fluxes, 1, 0, direction) - trimmed(fluxes, 0, 1, direction)


def strip_window(source, start, tile_width, fraction):
    window = lax.dynamic_slice_in_dim(source, start, tile_width + 1, source.ndim - 1)
    return (1.0 - fraction) * window[..., 1:] + fraction * window[..., :-1]


def row_barrel(rows, amounts, bit_count, sign):
    current = rows
    for level in range(bit_count):
        moved = jnp.roll(current, sign * 2**level, axis=2)
        taken = amounts // 2**level % 2 == 1
        current = jnp.where(taken[None, :, None], moved, current)
    return current


def sheared(strips, offset_cells, fraction):
    tile_width = strips.shape[3]
    total_cells = lax.axis_size("az") * tile_width
    backward = (total_cells - offset_cells - 1) % total_cells
    offsets = [offset_cells, backward]
    weights = [fraction, 1.0 - fraction]
    results = []
    offset_arr = jnp.stack(offsets)
    tiles = offset_arr // tile_width
    within = offset_arr % tile_width
    current = strips
    for level in range(lax.axis_size("az").bit_length() - 1):
        moved = passed_along(current, "az", 2**level)
        taken = tiles // 2**level % 2 == 1
        current = jnp.where(taken[:, None, None, None], moved, current)
    before = passed_along(current, "az", 1)
    joined = jnp.concatenate([before, current], axis=3)
    for side in range(2):
        start = tile_width - within[side] - 1
        results.append(strip_window(joined[side], start, tile_width, weights[side]))
    return jnp.stack(results)


def tendency(state, offset_cells, fraction, rotation):
    padded = padded_2(state, (("az", 2), ("rad", 1)), 2)
    columns = padded[:, :, 2:-2]
    strips = jnp.stack([columns[:, :2], columns[:, -2:]])
    ghosts = sheared(strips, offset_cells, fraction)
    radial = lax.axis_index("rad")
    lower_ghost = jnp.where(radial == 0, ghosts[0], columns[:, :2])
    upper_ghost = jnp.where(radial == lax.axis_size("rad") - 1, ghosts[1], columns[:, -2:])
    columns = jnp.concatenate([lower_ghost, columns[:, 2:-2], upper_ghost], axis=1)
    cycle_rows = padded[:, 2:-2, :]
    radial_div = sweep_axis(primitive(columns, 1), 1)
    azimuth_div = sweep_axis(primitive(cycle_rows, 2), 2)
    azimuth_div = jnp.stack([azimuth_div[0], azimuth_div[2], azimuth_div[1]])
    source = jnp.stack(
        [jnp.zeros_like(state[0]), 2.0 * rotation * state[2], -0.5 * rotation * state[1]]
    )
    return -(radial_div + azimuth_div) + source


def remap_rows(state, row_shift, row_frac):
    tile_width = state.shape[2]
    tiles = row_shift // tile_width
    within = row_shift % tile_width
    current = state
    for level in range(lax.axis_size("az").bit_length() - 1):
        moved = passed_along(current, "az", 2**level)
        taken = tiles // 2**level % 2 == 1
        current = jnp.where(taken[None, :, None], moved, current)
    before = passed_along(current, "az", 1)
    joined = jnp.concatenate([before, current], axis=2)
    lead = tile_width - within - 1
    aligned = row_barrel(joined, lead, tile_width.bit_length(), -1)
    weight = row_frac[None, :, None]
    return (1.0 - weight) * aligned[:, :, 1 : tile_width + 1] + weight * aligned[:, :, :tile_width]


def wide_ring(density, momentum, shear_shift, shear_frac, advect_shift, advect_frac, rotation):
    state = jnp.concatenate([density[None], momentum], axis=0)
    middle = state + TIME_STEP * tendency(state, shear_shift[0], shear_frac[0], rotation[0])
    final = 0.5 * state + 0.5 * (
        middle + TIME_STEP * tendency(middle, shear_shift[1], shear_frac[1], rotation[0])
    )
    remapped = remap_rows(final, advect_shift, advect_frac)
    return (remapped[0], remapped[1:])


def near(value):
    return pltpu.with_memory_space_constraint(value, pltpu.VMEM)


def per_device(density, momentum, shear_shift, shear_frac, advect_shift, advect_frac, rotation):
    tiles = lax.axis_size("az")
    radials = lax.axis_size("rad")
    rows, columns = density.shape
    sub = tiles * columns // LANES
    if sub != 8 or rows % 8:
        return wide_ring(
            density, momentum, shear_shift, shear_frac, advect_shift, advect_frac, rotation
        )

    def across(value, away):
        return lax.ppermute(value, "az", [(i, i ^ away) for i in range(tiles)])

    def along(value, steps):
        return lax.ppermute(value, "rad", [(i, (i + steps) % radials) for i in range(radials)])

    pieces = []
    for away in range(1, tiles):
        pieces += [across(density, away), across(momentum, away)]

    def edge(cut):
        parts = [density[None, cut], momentum[:, cut]]
        blocks = [jnp.concatenate(parts, axis=0)]
        for away in range(1, tiles):
            blocks.append(jnp.concatenate([pieces[2 * away - 2][None, cut], pieces[2 * away - 1][:, cut]], axis=0))
        return jnp.concatenate(blocks, axis=1)

    low = along(edge(slice(rows - HALO, rows)), 1)
    high = along(edge(slice(0, HALO)), -1)

    vmem = pl.BlockSpec(memory_space=pltpu.VMEM)
    smem = pl.BlockSpec(memory_space=pltpu.SMEM)
    operands = [near(p) for p in pieces] + [near(low), near(high)]
    return pl.pallas_call(
        functools.partial(step_kernel, (tiles, radials, rows, columns, sub)),
        out_shape=[
            jax.ShapeDtypeStruct(density.shape, density.dtype),
            jax.ShapeDtypeStruct(momentum.shape, momentum.dtype),
        ],
        in_specs=[smem] * 5 + [vmem] * (2 + len(operands)),
        out_specs=[vmem, vmem],
        scratch_shapes=[
            pltpu.VMEM((3, (rows + 16) * sub, LANES), jnp.float32),
            pltpu.VMEM((3, (rows + 4) * sub, LANES), jnp.float32),
            pltpu.VMEM((3, rows * sub, LANES), jnp.float32),
        ],
        compiler_params=pltpu.CompilerParams(vmem_limit_bytes=40 * 2**20),
    )(shear_shift, shear_frac, advect_shift, advect_frac, rotation, density, momentum, *operands)


def solution(mesh):
    in_specs = (
        P(("groups", "rad"), "az"),
        P("groups", "rad", "az"),
        P("groups"),
        P("groups"),
        P(("groups", "rad")),
        P(("groups", "rad")),
        P("groups"),
    )
    out_specs = (P(("groups", "rad"), "az"), P("groups", "rad", "az"))
    return jax.shard_map(
        per_device, mesh=mesh, in_specs=in_specs, out_specs=out_specs, check_vma=False
    )
```

```python
import functools

import jax
import jax.numpy as jnp
from jax import lax
from jax.experimental import pallas as pl
from jax.experimental.pallas import tpu as pltpu
from jax.sharding import PartitionSpec as P

TIME_STEP = 0.12
SOUND_SPEED = 1.0
LANES = 128
HALO = 4
EDGE_ORDER = (1, 3, 2)
INNER_ORDER = (2, 1, 3)
LOOPS = (1, 1, 2)


def turned(value, whole, part, lane):
    lanes = pltpu.roll(value, part, 1)
    same = pltpu.roll(lanes, whole, 0)
    before = pltpu.roll(same, 1, 0)
    return jnp.where(lane < part, before, same)


def previous(value, lane):
    lanes = pltpu.roll(value, 1, 1)
    return jnp.where(lane == 0, pltpu.roll(lanes, 1, 0), lanes)


def following(value, lane):
    lanes = pltpu.roll(value, LANES - 1, 1)
    return jnp.where(lane == LANES - 1, pltpu.roll(lanes, value.shape[0] - 1, 0), lanes)


def minmod(first, second):
    return jnp.maximum(jnp.minimum(second, 0.0), jnp.minimum(first, jnp.maximum(second, 0.0)))


def sums(left, right):
    signal = jnp.maximum(jnp.abs(left[1]), jnp.abs(right[1])) + 1.0
    lower = left[0] * (left[1] + signal)
    upper = right[0] * (right[1] - signal)
    return (
        lower + upper,
        (left[1] * lower + left[0]) + (right[1] * upper + right[0]),
        left[2] * lower + right[2] * upper,
    )


def minus(first, second):
    return tuple(a - b for a, b in zip(first, second))


def plus(first, second):
    return tuple(a + b for a, b in zip(first, second))


def primitives(state):
    inverse = 1.0 / state[0]
    return state[0], state[1] * inverse, state[2] * inverse


def azimuthal(whole):
    return whole[0], whole[2], whole[1]


def repeated(first, count, loops, body):
    each = count // loops

    def block(turn, carry):
        for step in range(each):
            body(first + turn * each + step)
        return carry

    if loops == 1:
        block(0, 0)
    else:
        lax.fori_loop(0, loops, block, 0)


def radial_sweep(load, emit, first, count, loops):
    def half_steps(above, below):
        return tuple(0.5 * (a - b) for a, b in zip(above, below))

    def advance(row, carry):
        whole = load(row)
        ahead = half_steps(whole, carry["whole"])
        slope = tuple(minmod(b, a) for b, a in zip(carry["ahead"], ahead))
        face = sums(carry["left"], minus(carry["whole"], slope))
        new = {"whole": whole, "ahead": ahead, "left": plus(carry["whole"], slope), "face": face}
        return new, minus(face, carry["face"])

    rows = [load(first - 2 + k) for k in range(4)]
    ahead = [half_steps(rows[k + 1], rows[k]) for k in range(3)]
    slopes = [tuple(minmod(b, a) for b, a in zip(ahead[k], ahead[k + 1])) for k in range(2)]
    carry = {
        "whole": rows[3],
        "ahead": ahead[2],
        "left": plus(rows[2], slopes[1]),
        "face": sums(plus(rows[1], slopes[0]), minus(rows[2], slopes[1])),
    }
    each = count // loops

    def block(turn, carry):
        for step in range(each):
            row = first + turn * each + step
            carry, across = advance(row + 2, carry)
            emit(row, across)
        return carry

    if loops == 1:
        block(0, carry)
    else:
        lax.fori_loop(0, loops, block, carry)


def split_kernel(*refs):
    density, momentum, edges, inner = refs[4:8]
    for given, kept in zip(refs[:4], refs[8:]):
        for place in range(given.shape[0]):
            kept[place] = given[place]
    rows = density.shape[0]
    for component, take in enumerate(
        (lambda cut: density[cut, :], lambda cut: momentum[0, cut, :], lambda cut: momentum[1, cut, :])
    ):
        edges[component, 0:HALO] = take(slice(0, HALO))
        edges[component, HALO : 2 * HALO] = take(slice(rows - HALO, rows))
        inner[component] = take(slice(HALO, rows - HALO))


def step_kernel(sizes, *refs):
    tiles, radials, rows, columns, sub = sizes
    per_tile = columns // LANES
    shear_shift, shear_frac, advect_shift, advect_frac, rotation = refs[:5]
    edges = refs[5 : 5 + tiles]
    inners = refs[5 + tiles : 5 + 2 * tiles]
    within, between, density_out, momentum_out, start, middle, remapped, whole, lower, upper, faces = refs[5 + 2 * tiles :]
    lane = lax.broadcasted_iota(jnp.int32, (sub, LANES), 1)
    az = lax.axis_index("az")
    radial = lax.axis_index("rad")
    main = 6
    end = main + rows + 4
    odd = radial % 2
    spot_within = jnp.where(odd == 1, 0, end + 2)
    spot_between = jnp.where(odd == 1, end + 2, 0)

    def place(value, component, row, tile, part):
        first = row * sub + tile * per_tile + part
        start[component, pl.ds(first, value.shape[0], stride=sub), :] = value

    for away in range(tiles):
        tile = az ^ away
        for part in range(per_tile):
            cut = slice(part * LANES, (part + 1) * LANES)
            for component in range(3):
                place(edges[away][component, 0:HALO, cut], component, main + 2, tile, part)
                place(edges[away][component, HALO : 2 * HALO, cut], component, end - 2 - HALO, tile, part)
                for row in range(0, rows - 2 * HALO, 8):
                    place(inners[away][component, row : row + 8, cut], component, main + 2 + HALO + row, tile, part)
                border = slice(HALO * away, HALO * away + HALO)
                place(within[component, border, cut], component, spot_within, tile, part)
                place(between[component, border, cut], component, spot_between, tile, part)

    def row_of(ref, component, row):
        return ref[component, pl.ds(row * sub if isinstance(row, int) else pl.multiple_of(row * sub, 8), sub), :]

    def state_of(ref, row):
        return tuple(row_of(ref, component, row) for component in range(3))

    def put(ref, row, state):
        for component in range(3):
            ref[component, pl.ds(row * sub if isinstance(row, int) else pl.multiple_of(row * sub, 8), sub), :] = state[component]

    at_low = radial == 0
    at_high = radial == radials - 1
    total = sub * LANES

    def from_below(state, section, here):
        shift = jnp.where(here, shear_shift[section], 0)
        weight = jnp.where(here, shear_frac[section], 0.0)
        moved = tuple(turned(s, shift // LANES, shift % LANES, lane) for s in state)
        return tuple((1.0 - weight) * m + weight * previous(m, lane) for m in moved)

    def from_above(state, section, here):
        shift = jnp.where(here, (total - shear_shift[section]) % total, 0)
        weight = jnp.where(here, shear_frac[section], 0.0)
        moved = tuple(turned(s, shift // LANES, shift % LANES, lane) for s in state)
        return tuple((1.0 - weight) * m + weight * following(m, lane) for m in moved)

    for k in range(2):
        put(start, main + k, from_below(state_of(start, 2 + k), 0, at_low))
        put(start, end - 2 + k, from_above(state_of(start, end + 2 + k), 0, at_high))
        put(start, 4 + k, from_above(state_of(start, main + 2 + k), 0, at_low))
        put(start, end + k, from_below(state_of(start, end - 4 + k), 0, at_high))

    spin = rotation[...]

    def changed(state, double):
        half_step = 0.5 * TIME_STEP
        return (
            state[0] - half_step * double[0],
            state[1] - half_step * double[1] + (2.0 * TIME_STEP) * spin * state[2],
            state[2] - half_step * double[2] - (0.5 * TIME_STEP) * spin * state[1],
        )

    def slopes(source, row):
        values = primitives(state_of(source, row))
        put(whole, row, values)
        normal = azimuthal(values)
        halves = tuple(0.5 * n for n in normal)
        slope = tuple(
            minmod(h - previous(h, lane), following(h, lane) - h) for h in halves
        )
        put(lower, row, plus(normal, slope))
        put(upper, row, minus(normal, slope))

    def meet(row):
        right = tuple(following(r, lane) for r in state_of(upper, row))
        put(faces, row, sums(state_of(lower, row), right))

    def turn(row):
        face = state_of(faces, row)
        return azimuthal(minus(face, tuple(previous(f, lane) for f in face)))

    def only(source, row):
        put(whole, row, primitives(state_of(source, row)))

    def emit_first(shift):
        def emit(row, across):
            put(middle, row + shift, changed(state_of(start, row), plus(across, turn(row))))
        return emit

    for row in (0, 1, 4, 5, main, main + 1, end - 2, end - 1, end, end + 1, end + 4, end + 5):
        only(start, row)
    for row in (2, 3, end + 2, end + 3):
        slopes(start, row)
    repeated(main + 2, rows, LOOPS[0], lambda row: slopes(start, row))
    for row in (2, 3, end + 2, end + 3):
        meet(row)
    repeated(main + 2, rows, LOOPS[1], meet)
    radial_sweep(lambda row: state_of(whole, row), emit_first(-2), 2, 2, 1)
    radial_sweep(lambda row: state_of(whole, row), emit_first(rows - end), end + 2, 2, 1)
    radial_sweep(lambda row: state_of(whole, row), emit_first(-main), main + 2, rows, LOOPS[2])

    for k in range(2):
        put(middle, k, from_below(state_of(middle, k), 1, at_low))
        put(middle, rows + 2 + k, from_above(state_of(middle, rows + 2 + k), 1, at_high))

    def emit_second(row, across):
        new = changed(state_of(middle, row), plus(across, turn(row)))
        old = state_of(start, row + main)
        final = tuple(0.5 * o + 0.5 * n for o, n in zip(old, new))
        shift = advect_shift[row - 2]
        weight = advect_frac[row - 2]
        moved = tuple(turned(f, shift // LANES, shift % LANES, lane) for f in final)
        put(remapped, row - 2, tuple((1.0 - weight) * m + weight * previous(m, lane) for m in moved))

    for row in (0, 1, rows + 2, rows + 3):
        only(middle, row)
    repeated(2, rows, LOOPS[0], lambda row: slopes(middle, row))
    repeated(2, rows, LOOPS[1], meet)
    radial_sweep(lambda row: state_of(whole, row), emit_second, 2, rows, LOOPS[2])

    for part in range(per_tile):
        cut = slice(part * LANES, (part + 1) * LANES)
        for row in range(0, rows, 8):
            first = row * sub + az * per_tile + part
            for component in range(3):
                value = remapped[component, pl.ds(first, 8, stride=sub), :]
                if component == 0:
                    density_out[row : row + 8, cut] = value
                else:
                    momentum_out[component - 1, row : row + 8, cut] = value


def passed_along(value, axis, steps):
    count = lax.axis_size(axis)
    pairs = [(source, (source + steps) % count) for source in range(count)]
    return lax.ppermute(value, axis, pairs)


def padded_2(block, sides, width):
    for axis, dim in sides:
        count = lax.axis_size(axis)
        forward = [(i, i + 1) for i in range(count - 1)]
        forward.append((count - 1, 0))
        backward = [(target, source) for source, target in forward]
        low = lax.ppermute(
            lax.slice_in_dim(block, block.shape[dim] - width, None, axis=dim), axis, forward
        )
        high = lax.ppermute(lax.slice_in_dim(block, 0, width, axis=dim), axis, backward)
        block = jnp.concatenate([low, block, high], axis=dim)
    return block


def signed_minmod(first, second):
    return 0.5 * (jnp.sign(first) + jnp.sign(second)) * jnp.minimum(jnp.abs(first), jnp.abs(second))


def trimmed(array, lower, upper, direction):
    return lax.slice_in_dim(array, lower, array.shape[direction] - upper, axis=direction)


def physical(state):
    mass_flux = state[0] * state[1]
    fluxes = jnp.stack(
        [
            mass_flux,
            mass_flux * state[1] + SOUND_SPEED * SOUND_SPEED * state[0],
            mass_flux * state[2],
        ]
    )
    conserved = jnp.stack([state[0], state[0] * state[1], state[0] * state[2]])
    return (fluxes, conserved)


def face_flux(left_state, right_state):
    left_flux, left_cons = physical(left_state)
    right_flux, right_cons = physical(right_state)
    signal = jnp.maximum(jnp.abs(left_state[1]), jnp.abs(right_state[1])) + SOUND_SPEED
    return 0.5 * (left_flux + right_flux) - 0.5 * signal * (right_cons - left_cons)


def primitive(conserved, normal):
    return jnp.stack(
        [conserved[0], conserved[normal] / conserved[0], conserved[3 - normal] / conserved[0]]
    )


def sweep_axis(prims, direction):
    slopes = signed_minmod(
        trimmed(prims, 1, 1, direction) - trimmed(prims, 0, 2, direction),
        trimmed(prims, 2, 0, direction) - trimmed(prims, 1, 1, direction),
    )
    left_state = trimmed(prims, 1, 2, direction) + 0.5 * trimmed(slopes, 0, 1, direction)
    right_state = trimmed(prims, 2, 1, direction) - 0.5 * trimmed(slopes, 1, 0, direction)
    fluxes = face_flux(left_state, right_state)
    return trimmed(fluxes, 1, 0, direction) - trimmed(fluxes, 0, 1, direction)


def strip_window(source, start, tile_width, fraction):
    window = lax.dynamic_slice_in_dim(source, start, tile_width + 1, source.ndim - 1)
    return (1.0 - fraction) * window[..., 1:] + fraction * window[..., :-1]


def row_barrel(rows, amounts, bit_count, sign):
    current = rows
    for level in range(bit_count):
        moved = jnp.roll(current, sign * 2**level, axis=2)
        taken = amounts // 2**level % 2 == 1
        current = jnp.where(taken[None, :, None], moved, current)
    return current


def sheared(strips, offset_cells, fraction):
    tile_width = strips.shape[3]
    total_cells = lax.axis_size("az") * tile_width
    backward = (total_cells - offset_cells - 1) % total_cells
    offsets = [offset_cells, backward]
    weights = [fraction, 1.0 - fraction]
    results = []
    offset_arr = jnp.stack(offsets)
    tiles = offset_arr // tile_width
    within = offset_arr % tile_width
    current = strips
    for level in range(lax.axis_size("az").bit_length() - 1):
        moved = passed_along(current, "az", 2**level)
        taken = tiles // 2**level % 2 == 1
        current = jnp.where(taken[:, None, None, None], moved, current)
    before = passed_along(current, "az", 1)
    joined = jnp.concatenate([before, current], axis=3)
    for side in range(2):
        start = tile_width - within[side] - 1
        results.append(strip_window(joined[side], start, tile_width, weights[side]))
    return jnp.stack(results)


def tendency(state, offset_cells, fraction, rotation):
    padded = padded_2(state, (("az", 2), ("rad", 1)), 2)
    columns = padded[:, :, 2:-2]
    strips = jnp.stack([columns[:, :2], columns[:, -2:]])
    ghosts = sheared(strips, offset_cells, fraction)
    radial = lax.axis_index("rad")
    lower_ghost = jnp.where(radial == 0, ghosts[0], columns[:, :2])
    upper_ghost = jnp.where(radial == lax.axis_size("rad") - 1, ghosts[1], columns[:, -2:])
    columns = jnp.concatenate([lower_ghost, columns[:, 2:-2], upper_ghost], axis=1)
    cycle_rows = padded[:, 2:-2, :]
    radial_div = sweep_axis(primitive(columns, 1), 1)
    azimuth_div = sweep_axis(primitive(cycle_rows, 2), 2)
    azimuth_div = jnp.stack([azimuth_div[0], azimuth_div[2], azimuth_div[1]])
    source = jnp.stack(
        [jnp.zeros_like(state[0]), 2.0 * rotation * state[2], -0.5 * rotation * state[1]]
    )
    return -(radial_div + azimuth_div) + source


def remap_rows(state, row_shift, row_frac):
    tile_width = state.shape[2]
    tiles = row_shift // tile_width
    within = row_shift % tile_width
    current = state
    for level in range(lax.axis_size("az").bit_length() - 1):
        moved = passed_along(current, "az", 2**level)
        taken = tiles // 2**level % 2 == 1
        current = jnp.where(taken[None, :, None], moved, current)
    before = passed_along(current, "az", 1)
    joined = jnp.concatenate([before, current], axis=2)
    lead = tile_width - within - 1
    aligned = row_barrel(joined, lead, tile_width.bit_length(), -1)
    weight = row_frac[None, :, None]
    return (1.0 - weight) * aligned[:, :, 1 : tile_width + 1] + weight * aligned[:, :, :tile_width]


def wide_ring(density, momentum, shear_shift, shear_frac, advect_shift, advect_frac, rotation):
    state = jnp.concatenate([density[None], momentum], axis=0)
    middle = state + TIME_STEP * tendency(state, shear_shift[0], shear_frac[0], rotation[0])
    final = 0.5 * state + 0.5 * (
        middle + TIME_STEP * tendency(middle, shear_shift[1], shear_frac[1], rotation[0])
    )
    remapped = remap_rows(final, advect_shift, advect_frac)
    return (remapped[0], remapped[1:])


def near(value):
    return pltpu.with_memory_space_constraint(value, pltpu.VMEM)


def per_device(density, momentum, shear_shift, shear_frac, advect_shift, advect_frac, rotation):
    tiles = lax.axis_size("az")
    radials = lax.axis_size("rad")
    rows, columns = density.shape
    sub = tiles * columns // LANES
    if tiles != 4 or sub != 8 or rows % 8 or radials % 2:
        return wide_ring(
            density, momentum, shear_shift, shear_frac, advect_shift, advect_frac, rotation
        )

    vmem = pl.BlockSpec(memory_space=pltpu.VMEM)
    smem = pl.BlockSpec(memory_space=pltpu.SMEM)

    def across(value, away):
        return lax.ppermute(value, "az", [(i, i ^ away) for i in range(tiles)])

    def swapped(value, lower):
        pairs = [((i + lower) % radials, (i + lower + 1) % radials) for i in range(0, radials, 2)]
        return lax.ppermute(value, "rad", pairs + [(b, a) for a, b in pairs])

    scalars = (shear_shift, shear_frac, advect_shift, advect_frac)
    spin = jnp.broadcast_to(rotation[:, None], (sub, LANES))
    edge, inner, *kept = pl.pallas_call(
        split_kernel,
        out_shape=[
            pltpu.VMEM((3, 2 * HALO, columns), jnp.float32),
            pltpu.VMEM((3, rows - 2 * HALO, columns), jnp.float32),
        ]
        + [pltpu.SMEM(s.shape, s.dtype) for s in scalars],
        in_specs=[smem] * 4 + [vmem] * 2,
        out_specs=[vmem] * 2 + [smem] * 4,
    )(*scalars, density, momentum)
    edges = {0: edge}
    inners = {0: inner}
    for away in EDGE_ORDER:
        edges[away] = across(edge, away)
    for away in INNER_ORDER:
        inners[away] = across(inner, away)
    top = jnp.concatenate([edges[away][:, :HALO] for away in range(tiles)], axis=1)
    bottom = jnp.concatenate([edges[away][:, HALO:] for away in range(tiles)], axis=1)
    odd = lax.axis_index("rad") % 2 == 1
    within = swapped(jnp.where(odd, top, bottom), 0)
    between = swapped(jnp.where(odd, bottom, top), 1)
    operands = [edges[away] for away in range(tiles)] + [inners[away] for away in range(tiles)]
    operands = [near(p) for p in [spin] + operands + [within, between]]
    return pl.pallas_call(
        functools.partial(step_kernel, (tiles, radials, rows, columns, sub)),
        out_shape=[
            jax.ShapeDtypeStruct(density.shape, density.dtype),
            jax.ShapeDtypeStruct(momentum.shape, momentum.dtype),
        ],
        in_specs=[smem] * 4 + [vmem] * len(operands),
        out_specs=[vmem, vmem],
        scratch_shapes=[
            pltpu.VMEM((3, (rows + 16) * sub, LANES), jnp.float32),
            pltpu.VMEM((3, (rows + 4) * sub, LANES), jnp.float32),
            pltpu.VMEM((3, rows * sub, LANES), jnp.float32),
        ]
        + [pltpu.VMEM((3, (rows + 16) * sub, LANES), jnp.float32)] * 4,
        compiler_params=pltpu.CompilerParams(vmem_limit_bytes=40 * 2**20),
    )(*kept, *operands)


def solution(mesh):
    in_specs = (
        P(("groups", "rad"), "az"),
        P("groups", "rad", "az"),
        P("groups"),
        P("groups"),
        P(("groups", "rad")),
        P(("groups", "rad")),
        P("groups"),
    )
    out_specs = (P(("groups", "rad"), "az"), P("groups", "rad", "az"))
    return jax.shard_map(
        per_device, mesh=mesh, in_specs=in_specs, out_specs=out_specs, check_vma=False
    )
```

```python
import functools

import jax
import jax.numpy as jnp
from jax import lax
from jax.experimental import pallas as pl
from jax.experimental.pallas import tpu as pltpu
from jax.sharding import PartitionSpec as P

TIME_STEP = 0.12
SOUND_SPEED = 1.0
LANES = 128
HALO = 4
EDGE_ORDER = (1, 3, 2)
INNER_ORDER = (2, 1, 3)
LOOPS = (1, 1, 2)


def turned(value, whole, part, lane):
    lanes = pltpu.roll(value, part, 1)
    same = pltpu.roll(lanes, whole, 0)
    before = pltpu.roll(same, 1, 0)
    return jnp.where(lane < part, before, same)


def previous(value, lane):
    lanes = pltpu.roll(value, 1, 1)
    return jnp.where(lane == 0, pltpu.roll(lanes, 1, 0), lanes)


def following(value, lane):
    lanes = pltpu.roll(value, LANES - 1, 1)
    return jnp.where(lane == LANES - 1, pltpu.roll(lanes, value.shape[0] - 1, 0), lanes)


def minmod(first, second):
    return jnp.maximum(jnp.minimum(second, 0.0), jnp.minimum(first, jnp.maximum(second, 0.0)))


def sums(left, right):
    signal = jnp.maximum(jnp.abs(left[1]), jnp.abs(right[1])) + 1.0
    lower = left[0] * (left[1] + signal)
    upper = right[0] * (right[1] - signal)
    return (
        lower + upper,
        (left[1] * lower + left[0]) + (right[1] * upper + right[0]),
        left[2] * lower + right[2] * upper,
    )


def minus(first, second):
    return tuple(a - b for a, b in zip(first, second))


def plus(first, second):
    return tuple(a + b for a, b in zip(first, second))


def primitives(state):
    inverse = 1.0 / state[0]
    return state[0], state[1] * inverse, state[2] * inverse


def azimuthal(whole):
    return whole[0], whole[2], whole[1]


def repeated(first, count, loops, body):
    each = count // loops

    def block(turn, carry):
        for step in range(each):
            body(first + turn * each + step)
        return carry

    if loops == 1:
        block(0, 0)
    else:
        lax.fori_loop(0, loops, block, 0)


def radial_sweep(load, emit, first, count, loops):
    def half_steps(above, below):
        return tuple(0.5 * (a - b) for a, b in zip(above, below))

    def advance(row, carry):
        whole = load(row)
        ahead = half_steps(whole, carry["whole"])
        slope = tuple(minmod(b, a) for b, a in zip(carry["ahead"], ahead))
        face = sums(carry["left"], minus(carry["whole"], slope))
        new = {"whole": whole, "ahead": ahead, "left": plus(carry["whole"], slope), "face": face}
        return new, minus(face, carry["face"])

    rows = [load(first - 2 + k) for k in range(4)]
    ahead = [half_steps(rows[k + 1], rows[k]) for k in range(3)]
    slopes = [tuple(minmod(b, a) for b, a in zip(ahead[k], ahead[k + 1])) for k in range(2)]
    carry = {
        "whole": rows[3],
        "ahead": ahead[2],
        "left": plus(rows[2], slopes[1]),
        "face": sums(plus(rows[1], slopes[0]), minus(rows[2], slopes[1])),
    }
    each = count // loops

    def block(turn, carry):
        for step in range(each):
            row = first + turn * each + step
            carry, across = advance(row + 2, carry)
            emit(row, across)
        return carry

    if loops == 1:
        block(0, carry)
    else:
        lax.fori_loop(0, loops, block, carry)


def split_kernel(*refs):
    advect_frac, density, momentum, edges, inner, weights = refs[3:9]
    for given, kept in zip(refs[:3], refs[9:]):
        for place in range(given.shape[0]):
            kept[place] = given[place]
    rows = density.shape[0]
    for component, take in enumerate(
        (lambda cut: density[cut, :], lambda cut: momentum[0, cut, :], lambda cut: momentum[1, cut, :])
    ):
        edges[component, 0:HALO] = take(slice(0, HALO))
        edges[component, HALO : 2 * HALO] = take(slice(rows - HALO, rows))
        inner[component] = take(slice(HALO, rows - HALO))
    for row in range(rows):
        weights[row : row + 1, :] = jnp.full((1, LANES), advect_frac[row], jnp.float32)


def step_kernel(sizes, *refs):
    tiles, radials, rows, columns, sub = sizes
    per_tile = columns // LANES
    shear_shift, shear_frac, advect_shift, weights, rotation = refs[:5]
    edges = refs[5 : 5 + tiles]
    inners = refs[5 + tiles : 5 + 2 * tiles]
    within, between, density_out, momentum_out, start, middle, remapped, whole, lower, upper, faces = refs[5 + 2 * tiles :]
    lane = lax.broadcasted_iota(jnp.int32, (sub, LANES), 1)
    az = lax.axis_index("az")
    radial = lax.axis_index("rad")
    main = 6
    end = main + rows + 4
    odd = radial % 2
    spot_within = jnp.where(odd == 1, 0, end + 2)
    spot_between = jnp.where(odd == 1, end + 2, 0)

    def place(value, component, row, tile, part):
        first = row * sub + tile * per_tile + part
        start[component, pl.ds(first, value.shape[0], stride=sub), :] = value

    for away in range(tiles):
        tile = az ^ away
        for part in range(per_tile):
            cut = slice(part * LANES, (part + 1) * LANES)
            for component in range(3):
                place(edges[away][component, 0:HALO, cut], component, main + 2, tile, part)
                place(edges[away][component, HALO : 2 * HALO, cut], component, end - 2 - HALO, tile, part)
                for row in range(0, rows - 2 * HALO, 8):
                    place(inners[away][component, row : row + 8, cut], component, main + 2 + HALO + row, tile, part)
                border = slice(HALO * away, HALO * away + HALO)
                place(within[component, border, cut], component, spot_within, tile, part)
                place(between[component, border, cut], component, spot_between, tile, part)

    def row_of(ref, component, row):
        return ref[component, pl.ds(row * sub if isinstance(row, int) else pl.multiple_of(row * sub, 8), sub), :]

    def state_of(ref, row):
        return tuple(row_of(ref, component, row) for component in range(3))

    def put(ref, row, state):
        for component in range(3):
            ref[component, pl.ds(row * sub if isinstance(row, int) else pl.multiple_of(row * sub, 8), sub), :] = state[component]

    at_low = radial == 0
    at_high = radial == radials - 1
    total = sub * LANES

    def from_below(state, section, here):
        shift = jnp.where(here, shear_shift[section], 0)
        weight = jnp.where(here, shear_frac[section], 0.0)
        moved = tuple(turned(s, shift // LANES, shift % LANES, lane) for s in state)
        return tuple((1.0 - weight) * m + weight * previous(m, lane) for m in moved)

    def from_above(state, section, here):
        shift = jnp.where(here, (total - shear_shift[section]) % total, 0)
        weight = jnp.where(here, shear_frac[section], 0.0)
        moved = tuple(turned(s, shift // LANES, shift % LANES, lane) for s in state)
        return tuple((1.0 - weight) * m + weight * following(m, lane) for m in moved)

    for k in range(2):
        put(start, main + k, from_below(state_of(start, 2 + k), 0, at_low))
        put(start, end - 2 + k, from_above(state_of(start, end + 2 + k), 0, at_high))
        put(start, 4 + k, from_above(state_of(start, main + 2 + k), 0, at_low))
        put(start, end + k, from_below(state_of(start, end - 4 + k), 0, at_high))

    spin = rotation[...]

    def changed(state, double):
        half_step = 0.5 * TIME_STEP
        return (
            state[0] - half_step * double[0],
            state[1] - half_step * double[1] + (2.0 * TIME_STEP) * spin * state[2],
            state[2] - half_step * double[2] - (0.5 * TIME_STEP) * spin * state[1],
        )

    def slopes(source, row):
        values = primitives(state_of(source, row))
        put(whole, row, values)
        normal = azimuthal(values)
        halves = tuple(0.5 * n for n in normal)
        slope = tuple(
            minmod(h - previous(h, lane), following(h, lane) - h) for h in halves
        )
        put(lower, row, plus(normal, slope))
        put(upper, row, minus(normal, slope))

    def meet(row):
        right = tuple(following(r, lane) for r in state_of(upper, row))
        put(faces, row, sums(state_of(lower, row), right))

    def turn(row):
        face = state_of(faces, row)
        return azimuthal(minus(face, tuple(previous(f, lane) for f in face)))

    def only(source, row):
        put(whole, row, primitives(state_of(source, row)))

    def emit_first(shift):
        def emit(row, across):
            put(middle, row + shift, changed(state_of(start, row), plus(across, turn(row))))
        return emit

    for row in (0, 1, 4, 5, main, main + 1, end - 2, end - 1, end, end + 1, end + 4, end + 5):
        only(start, row)
    for row in (2, 3, end + 2, end + 3):
        slopes(start, row)
    repeated(main + 2, rows, LOOPS[0], lambda row: slopes(start, row))
    for row in (2, 3, end + 2, end + 3):
        meet(row)
    repeated(main + 2, rows, LOOPS[1], meet)
    radial_sweep(lambda row: state_of(whole, row), emit_first(-2), 2, 2, 1)
    radial_sweep(lambda row: state_of(whole, row), emit_first(rows - end), end + 2, 2, 1)
    radial_sweep(lambda row: state_of(whole, row), emit_first(-main), main + 2, rows, LOOPS[2])

    for k in range(2):
        put(middle, k, from_below(state_of(middle, k), 1, at_low))
        put(middle, rows + 2 + k, from_above(state_of(middle, rows + 2 + k), 1, at_high))

    def emit_second(row, across):
        new = changed(state_of(middle, row), plus(across, turn(row)))
        old = state_of(start, row + main)
        final = tuple(0.5 * (o + n) for o, n in zip(old, new))
        shift = advect_shift[row - 2]
        put(remapped, row - 2, tuple(turned(f, shift // LANES, shift % LANES, lane) for f in final))

    for row in (0, 1, rows + 2, rows + 3):
        only(middle, row)
    repeated(2, rows, LOOPS[0], lambda row: slopes(middle, row))
    repeated(2, rows, LOOPS[1], meet)
    radial_sweep(lambda row: state_of(whole, row), emit_second, 2, rows, LOOPS[2])

    for row in range(0, rows, 8):
        weight = weights[row : row + 8, :]
        for component in range(3):
            spots = [(az * per_tile + part + sub - 1) % sub for part in range(per_tile + 1)]
            tiles_here = [remapped[component, pl.ds(row * sub + spot, 8, stride=sub), :] for spot in spots]
            moved = [pltpu.roll(t, 1, 1) for t in tiles_here]
            for part in range(per_tile):
                cut = slice(part * LANES, (part + 1) * LANES)
                before = jnp.where(lane == 0, moved[part], moved[part + 1])
                value = (1.0 - weight) * tiles_here[part + 1] + weight * before
                if component == 0:
                    density_out[row : row + 8, cut] = value
                else:
                    momentum_out[component - 1, row : row + 8, cut] = value


def passed_along(value, axis, steps):
    count = lax.axis_size(axis)
    pairs = [(source, (source + steps) % count) for source in range(count)]
    return lax.ppermute(value, axis, pairs)


def padded_2(block, sides, width):
    for axis, dim in sides:
        count = lax.axis_size(axis)
        forward = [(i, i + 1) for i in range(count - 1)]
        forward.append((count - 1, 0))
        backward = [(target, source) for source, target in forward]
        low = lax.ppermute(
            lax.slice_in_dim(block, block.shape[dim] - width, None, axis=dim), axis, forward
        )
        high = lax.ppermute(lax.slice_in_dim(block, 0, width, axis=dim), axis, backward)
        block = jnp.concatenate([low, block, high], axis=dim)
    return block


def signed_minmod(first, second):
    return 0.5 * (jnp.sign(first) + jnp.sign(second)) * jnp.minimum(jnp.abs(first), jnp.abs(second))


def trimmed(array, lower, upper, direction):
    return lax.slice_in_dim(array, lower, array.shape[direction] - upper, axis=direction)


def physical(state):
    mass_flux = state[0] * state[1]
    fluxes = jnp.stack(
        [
            mass_flux,
            mass_flux * state[1] + SOUND_SPEED * SOUND_SPEED * state[0],
            mass_flux * state[2],
        ]
    )
    conserved = jnp.stack([state[0], state[0] * state[1], state[0] * state[2]])
    return (fluxes, conserved)


def face_flux(left_state, right_state):
    left_flux, left_cons = physical(left_state)
    right_flux, right_cons = physical(right_state)
    signal = jnp.maximum(jnp.abs(left_state[1]), jnp.abs(right_state[1])) + SOUND_SPEED
    return 0.5 * (left_flux + right_flux) - 0.5 * signal * (right_cons - left_cons)


def primitive(conserved, normal):
    return jnp.stack(
        [conserved[0], conserved[normal] / conserved[0], conserved[3 - normal] / conserved[0]]
    )


def sweep_axis(prims, direction):
    slopes = signed_minmod(
        trimmed(prims, 1, 1, direction) - trimmed(prims, 0, 2, direction),
        trimmed(prims, 2, 0, direction) - trimmed(prims, 1, 1, direction),
    )
    left_state = trimmed(prims, 1, 2, direction) + 0.5 * trimmed(slopes, 0, 1, direction)
    right_state = trimmed(prims, 2, 1, direction) - 0.5 * trimmed(slopes, 1, 0, direction)
    fluxes = face_flux(left_state, right_state)
    return trimmed(fluxes, 1, 0, direction) - trimmed(fluxes, 0, 1, direction)


def strip_window(source, start, tile_width, fraction):
    window = lax.dynamic_slice_in_dim(source, start, tile_width + 1, source.ndim - 1)
    return (1.0 - fraction) * window[..., 1:] + fraction * window[..., :-1]


def row_barrel(rows, amounts, bit_count, sign):
    current = rows
    for level in range(bit_count):
        moved = jnp.roll(current, sign * 2**level, axis=2)
        taken = amounts // 2**level % 2 == 1
        current = jnp.where(taken[None, :, None], moved, current)
    return current


def sheared(strips, offset_cells, fraction):
    tile_width = strips.shape[3]
    total_cells = lax.axis_size("az") * tile_width
    backward = (total_cells - offset_cells - 1) % total_cells
    offsets = [offset_cells, backward]
    weights = [fraction, 1.0 - fraction]
    results = []
    offset_arr = jnp.stack(offsets)
    tiles = offset_arr // tile_width
    within = offset_arr % tile_width
    current = strips
    for level in range(lax.axis_size("az").bit_length() - 1):
        moved = passed_along(current, "az", 2**level)
        taken = tiles // 2**level % 2 == 1
        current = jnp.where(taken[:, None, None, None], moved, current)
    before = passed_along(current, "az", 1)
    joined = jnp.concatenate([before, current], axis=3)
    for side in range(2):
        start = tile_width - within[side] - 1
        results.append(strip_window(joined[side], start, tile_width, weights[side]))
    return jnp.stack(results)


def tendency(state, offset_cells, fraction, rotation):
    padded = padded_2(state, (("az", 2), ("rad", 1)), 2)
    columns = padded[:, :, 2:-2]
    strips = jnp.stack([columns[:, :2], columns[:, -2:]])
    ghosts = sheared(strips, offset_cells, fraction)
    radial = lax.axis_index("rad")
    lower_ghost = jnp.where(radial == 0, ghosts[0], columns[:, :2])
    upper_ghost = jnp.where(radial == lax.axis_size("rad") - 1, ghosts[1], columns[:, -2:])
    columns = jnp.concatenate([lower_ghost, columns[:, 2:-2], upper_ghost], axis=1)
    cycle_rows = padded[:, 2:-2, :]
    radial_div = sweep_axis(primitive(columns, 1), 1)
    azimuth_div = sweep_axis(primitive(cycle_rows, 2), 2)
    azimuth_div = jnp.stack([azimuth_div[0], azimuth_div[2], azimuth_div[1]])
    source = jnp.stack(
        [jnp.zeros_like(state[0]), 2.0 * rotation * state[2], -0.5 * rotation * state[1]]
    )
    return -(radial_div + azimuth_div) + source


def remap_rows(state, row_shift, row_frac):
    tile_width = state.shape[2]
    tiles = row_shift // tile_width
    within = row_shift % tile_width
    current = state
    for level in range(lax.axis_size("az").bit_length() - 1):
        moved = passed_along(current, "az", 2**level)
        taken = tiles // 2**level % 2 == 1
        current = jnp.where(taken[None, :, None], moved, current)
    before = passed_along(current, "az", 1)
    joined = jnp.concatenate([before, current], axis=2)
    lead = tile_width - within - 1
    aligned = row_barrel(joined, lead, tile_width.bit_length(), -1)
    weight = row_frac[None, :, None]
    return (1.0 - weight) * aligned[:, :, 1 : tile_width + 1] + weight * aligned[:, :, :tile_width]


def wide_ring(density, momentum, shear_shift, shear_frac, advect_shift, advect_frac, rotation):
    state = jnp.concatenate([density[None], momentum], axis=0)
    middle = state + TIME_STEP * tendency(state, shear_shift[0], shear_frac[0], rotation[0])
    final = 0.5 * state + 0.5 * (
        middle + TIME_STEP * tendency(middle, shear_shift[1], shear_frac[1], rotation[0])
    )
    remapped = remap_rows(final, advect_shift, advect_frac)
    return (remapped[0], remapped[1:])


def near(value):
    return pltpu.with_memory_space_constraint(value, pltpu.VMEM)


def per_device(density, momentum, shear_shift, shear_frac, advect_shift, advect_frac, rotation):
    tiles = lax.axis_size("az")
    radials = lax.axis_size("rad")
    rows, columns = density.shape
    sub = tiles * columns // LANES
    if tiles != 4 or sub != 8 or rows % 8 or radials % 2:
        return wide_ring(
            density, momentum, shear_shift, shear_frac, advect_shift, advect_frac, rotation
        )

    vmem = pl.BlockSpec(memory_space=pltpu.VMEM)
    smem = pl.BlockSpec(memory_space=pltpu.SMEM)

    def across(value, away):
        return lax.ppermute(value, "az", [(i, i ^ away) for i in range(tiles)])

    def swapped(value, lower):
        pairs = [((i + lower) % radials, (i + lower + 1) % radials) for i in range(0, radials, 2)]
        return lax.ppermute(value, "rad", pairs + [(b, a) for a, b in pairs])

    scalars = (shear_shift, shear_frac, advect_shift, advect_frac)
    spin = jnp.broadcast_to(rotation[:, None], (sub, LANES))
    edge, inner, weights, *kept = pl.pallas_call(
        split_kernel,
        out_shape=[
            pltpu.VMEM((3, 2 * HALO, columns), jnp.float32),
            pltpu.VMEM((3, rows - 2 * HALO, columns), jnp.float32),
            pltpu.VMEM((rows, LANES), jnp.float32),
        ]
        + [pltpu.SMEM(s.shape, s.dtype) for s in scalars[:3]],
        in_specs=[smem] * 4 + [vmem] * 2,
        out_specs=[vmem] * 3 + [smem] * 3,
    )(*scalars, density, momentum)
    edges = {0: edge}
    inners = {0: inner}
    for away in EDGE_ORDER:
        edges[away] = across(edge, away)
    for away in INNER_ORDER:
        inners[away] = across(inner, away)
    top = jnp.concatenate([edges[away][:, :HALO] for away in range(tiles)], axis=1)
    bottom = jnp.concatenate([edges[away][:, HALO:] for away in range(tiles)], axis=1)
    odd = lax.axis_index("rad") % 2 == 1
    between = swapped(jnp.where(odd, bottom, top), 1)
    within = swapped(jnp.where(odd, top, bottom), 0)
    operands = [edges[away] for away in range(tiles)] + [inners[away] for away in range(tiles)]
    operands = [near(p) for p in [weights, spin] + operands + [within, between]]
    return pl.pallas_call(
        functools.partial(step_kernel, (tiles, radials, rows, columns, sub)),
        out_shape=[
            jax.ShapeDtypeStruct(density.shape, density.dtype),
            jax.ShapeDtypeStruct(momentum.shape, momentum.dtype),
        ],
        in_specs=[smem] * 3 + [vmem] * len(operands),
        out_specs=[vmem, vmem],
        scratch_shapes=[
            pltpu.VMEM((3, (rows + 17) * sub, LANES), jnp.float32),
            pltpu.VMEM((3, (rows + 4) * sub, LANES), jnp.float32),
            pltpu.VMEM((3, (rows + 1) * sub, LANES), jnp.float32),
        ]
        + [pltpu.VMEM((3, (rows + 16) * sub, LANES), jnp.float32)] * 4,
        compiler_params=pltpu.CompilerParams(vmem_limit_bytes=40 * 2**20),
    )(*kept, *operands)


def solution(mesh):
    in_specs = (
        P(("groups", "rad"), "az"),
        P("groups", "rad", "az"),
        P("groups"),
        P("groups"),
        P(("groups", "rad")),
        P(("groups", "rad")),
        P("groups"),
    )
    out_specs = (P(("groups", "rad"), "az"), P("groups", "rad", "az"))
    return jax.shard_map(
        per_device, mesh=mesh, in_specs=in_specs, out_specs=out_specs, check_vma=False
    )
```

```python
import functools

import jax
import jax.numpy as jnp
from jax import lax
from jax.experimental import pallas as pl
from jax.experimental.pallas import tpu as pltpu
from jax.sharding import PartitionSpec as P

TIME_STEP = 0.12
SOUND_SPEED = 1.0
LANES = 128
HALO = 4
EDGE_ORDER = (1, 3, 2)
INNER_ORDER = (2, 1, 3)
LOOPS = (1, 1, 2)


def turned(value, whole, part, lane):
    lanes = pltpu.roll(value, part, 1)
    same = pltpu.roll(lanes, whole, 0)
    before = pltpu.roll(same, 1, 0)
    return jnp.where(lane < part, before, same)


def previous(value, lane):
    lanes = pltpu.roll(value, 1, 1)
    return jnp.where(lane == 0, pltpu.roll(lanes, 1, 0), lanes)


def following(value, lane):
    lanes = pltpu.roll(value, LANES - 1, 1)
    return jnp.where(lane == LANES - 1, pltpu.roll(lanes, value.shape[0] - 1, 0), lanes)


def minmod(first, second):
    return jnp.maximum(jnp.minimum(second, 0.0), jnp.minimum(first, jnp.maximum(second, 0.0)))


def sums(left, right):
    signal = jnp.maximum(jnp.abs(left[1]), jnp.abs(right[1])) + 1.0
    lower = left[0] * (left[1] + signal)
    upper = right[0] * (right[1] - signal)
    return (
        lower + upper,
        (left[1] * lower + left[0]) + (right[1] * upper + right[0]),
        left[2] * lower + right[2] * upper,
    )


def minus(first, second):
    return tuple(a - b for a, b in zip(first, second))


def plus(first, second):
    return tuple(a + b for a, b in zip(first, second))


def primitives(state):
    inverse = 1.0 / state[0]
    return state[0], state[1] * inverse, state[2] * inverse


def azimuthal(whole):
    return whole[0], whole[2], whole[1]


def repeated(first, count, loops, body):
    each = count // loops

    def block(turn, carry):
        for step in range(each):
            body(first + turn * each + step)
        return carry

    if loops == 1:
        block(0, 0)
    else:
        lax.fori_loop(0, loops, block, 0)


def radial_sweep(load, emit, first, count, loops):
    def half_steps(above, below):
        return tuple(0.5 * (a - b) for a, b in zip(above, below))

    def advance(row, carry):
        whole = load(row)
        ahead = half_steps(whole, carry["whole"])
        slope = tuple(minmod(b, a) for b, a in zip(carry["ahead"], ahead))
        face = sums(carry["left"], minus(carry["whole"], slope))
        new = {"whole": whole, "ahead": ahead, "left": plus(carry["whole"], slope), "face": face}
        return new, minus(face, carry["face"])

    rows = [load(first - 2 + k) for k in range(4)]
    ahead = [half_steps(rows[k + 1], rows[k]) for k in range(3)]
    slopes = [tuple(minmod(b, a) for b, a in zip(ahead[k], ahead[k + 1])) for k in range(2)]
    carry = {
        "whole": rows[3],
        "ahead": ahead[2],
        "left": plus(rows[2], slopes[1]),
        "face": sums(plus(rows[1], slopes[0]), minus(rows[2], slopes[1])),
    }
    each = count // loops

    def block(turn, carry):
        for step in range(each):
            row = first + turn * each + step
            carry, across = advance(row + 2, carry)
            emit(row, across)
        return carry

    if loops == 1:
        block(0, carry)
    else:
        lax.fori_loop(0, loops, block, carry)


def split_kernel(*refs):
    advect_frac, density, momentum, edges, inner, weights = refs[3:9]
    for given, kept in zip(refs[:3], refs[9:]):
        for place in range(given.shape[0]):
            kept[place] = given[place]
    rows = density.shape[0]
    for component, take in enumerate(
        (lambda cut: density[cut, :], lambda cut: momentum[0, cut, :], lambda cut: momentum[1, cut, :])
    ):
        edges[component, 0:HALO] = take(slice(0, HALO))
        edges[component, HALO : 2 * HALO] = take(slice(rows - HALO, rows))
        inner[component] = take(slice(HALO, rows - HALO))
    for row in range(rows):
        weights[row : row + 1, :] = jnp.full((1, LANES), advect_frac[row], jnp.float32)


def step_kernel(sizes, *refs):
    tiles, radials, rows, columns, sub = sizes
    per_tile = columns // LANES
    shear_shift, shear_frac, advect_shift, weights, rotation = refs[:5]
    edges = dict(zip((0,) + EDGE_ORDER, refs[5 : 5 + tiles]))
    inners = dict(zip((0,) + INNER_ORDER, refs[5 + tiles : 5 + 2 * tiles]))
    within, between, density_out, momentum_out, start, middle, remapped, whole, lower, upper, faces = refs[5 + 2 * tiles :]
    lane = lax.broadcasted_iota(jnp.int32, (sub, LANES), 1)
    az = lax.axis_index("az")
    radial = lax.axis_index("rad")
    main = 6
    end = main + rows + 4
    odd = radial % 2
    spot_within = jnp.where(odd == 1, 0, end + 2)
    spot_between = jnp.where(odd == 1, end + 2, 0)

    def place(value, component, row, tile, part):
        first = row * sub + tile * per_tile + part
        start[component, pl.ds(first, value.shape[0], stride=sub), :] = value

    for away in range(tiles):
        tile = az ^ away
        for part in range(per_tile):
            cut = slice(part * LANES, (part + 1) * LANES)
            for component in range(3):
                place(edges[away][component, 0:HALO, cut], component, main + 2, tile, part)
                place(edges[away][component, HALO : 2 * HALO, cut], component, end - 2 - HALO, tile, part)
                for row in range(0, rows - 2 * HALO, 8):
                    place(inners[away][component, row : row + 8, cut], component, main + 2 + HALO + row, tile, part)
                border = slice(HALO * away, HALO * away + HALO)
                place(within[component, border, cut], component, spot_within, tile, part)
                place(between[component, border, cut], component, spot_between, tile, part)

    def row_of(ref, component, row):
        return ref[component, pl.ds(row * sub if isinstance(row, int) else pl.multiple_of(row * sub, 8), sub), :]

    def state_of(ref, row):
        return tuple(row_of(ref, component, row) for component in range(3))

    def put(ref, row, state):
        for component in range(3):
            ref[component, pl.ds(row * sub if isinstance(row, int) else pl.multiple_of(row * sub, 8), sub), :] = state[component]

    at_low = radial == 0
    at_high = radial == radials - 1
    total = sub * LANES

    def from_below(state, section, here):
        shift = jnp.where(here, shear_shift[section], 0)
        weight = jnp.where(here, shear_frac[section], 0.0)
        moved = tuple(turned(s, shift // LANES, shift % LANES, lane) for s in state)
        return tuple((1.0 - weight) * m + weight * previous(m, lane) for m in moved)

    def from_above(state, section, here):
        shift = jnp.where(here, (total - shear_shift[section]) % total, 0)
        weight = jnp.where(here, shear_frac[section], 0.0)
        moved = tuple(turned(s, shift // LANES, shift % LANES, lane) for s in state)
        return tuple((1.0 - weight) * m + weight * following(m, lane) for m in moved)

    for k in range(2):
        put(start, main + k, from_below(state_of(start, 2 + k), 0, at_low))
        put(start, end - 2 + k, from_above(state_of(start, end + 2 + k), 0, at_high))
        put(start, 4 + k, from_above(state_of(start, main + 2 + k), 0, at_low))
        put(start, end + k, from_below(state_of(start, end - 4 + k), 0, at_high))

    spin = rotation[...]

    def changed(state, double):
        half_step = 0.5 * TIME_STEP
        return (
            state[0] - half_step * double[0],
            state[1] - half_step * double[1] + (2.0 * TIME_STEP) * spin * state[2],
            state[2] - half_step * double[2] - (0.5 * TIME_STEP) * spin * state[1],
        )

    def slopes(source, row):
        values = primitives(state_of(source, row))
        put(whole, row, values)
        normal = azimuthal(values)
        halves = tuple(0.5 * n for n in normal)
        slope = tuple(
            minmod(h - previous(h, lane), following(h, lane) - h) for h in halves
        )
        put(lower, row, plus(normal, slope))
        put(upper, row, minus(normal, slope))

    def meet(row):
        right = tuple(following(r, lane) for r in state_of(upper, row))
        put(faces, row, sums(state_of(lower, row), right))

    def turn(row):
        face = state_of(faces, row)
        return azimuthal(minus(face, tuple(previous(f, lane) for f in face)))

    def only(source, row):
        put(whole, row, primitives(state_of(source, row)))

    def emit_first(shift):
        def emit(row, across):
            put(middle, row + shift, changed(state_of(start, row), plus(across, turn(row))))
        return emit

    for row in (0, 1, 4, 5, main, main + 1, end - 2, end - 1, end, end + 1, end + 4, end + 5):
        only(start, row)
    for row in (2, 3, end + 2, end + 3):
        slopes(start, row)
    repeated(main + 2, rows, LOOPS[0], lambda row: slopes(start, row))
    for row in (2, 3, end + 2, end + 3):
        meet(row)
    repeated(main + 2, rows, LOOPS[1], meet)
    radial_sweep(lambda row: state_of(whole, row), emit_first(-2), 2, 2, 1)
    radial_sweep(lambda row: state_of(whole, row), emit_first(rows - end), end + 2, 2, 1)
    radial_sweep(lambda row: state_of(whole, row), emit_first(-main), main + 2, rows, LOOPS[2])

    for k in range(2):
        put(middle, k, from_below(state_of(middle, k), 1, at_low))
        put(middle, rows + 2 + k, from_above(state_of(middle, rows + 2 + k), 1, at_high))

    def emit_second(row, across):
        new = changed(state_of(middle, row), plus(across, turn(row)))
        old = state_of(start, row + main)
        final = tuple(0.5 * (o + n) for o, n in zip(old, new))
        shift = advect_shift[row - 2]
        put(remapped, row - 2, tuple(turned(f, shift // LANES, shift % LANES, lane) for f in final))

    for row in (0, 1, rows + 2, rows + 3):
        only(middle, row)
    repeated(2, rows, LOOPS[0], lambda row: slopes(middle, row))
    repeated(2, rows, LOOPS[1], meet)
    radial_sweep(lambda row: state_of(whole, row), emit_second, 2, rows, LOOPS[2])

    for row in range(0, rows, 8):
        weight = weights[row : row + 8, :]
        for component in range(3):
            spots = [(az * per_tile + part + sub - 1) % sub for part in range(per_tile + 1)]
            tiles_here = [remapped[component, pl.ds(row * sub + spot, 8, stride=sub), :] for spot in spots]
            moved = [pltpu.roll(t, 1, 1) for t in tiles_here]
            for part in range(per_tile):
                cut = slice(part * LANES, (part + 1) * LANES)
                before = jnp.where(lane == 0, moved[part], moved[part + 1])
                value = (1.0 - weight) * tiles_here[part + 1] + weight * before
                if component == 0:
                    density_out[row : row + 8, cut] = value
                else:
                    momentum_out[component - 1, row : row + 8, cut] = value


def passed_along(value, axis, steps):
    count = lax.axis_size(axis)
    pairs = [(source, (source + steps) % count) for source in range(count)]
    return lax.ppermute(value, axis, pairs)


def padded_2(block, sides, width):
    for axis, dim in sides:
        count = lax.axis_size(axis)
        forward = [(i, i + 1) for i in range(count - 1)]
        forward.append((count - 1, 0))
        backward = [(target, source) for source, target in forward]
        low = lax.ppermute(
            lax.slice_in_dim(block, block.shape[dim] - width, None, axis=dim), axis, forward
        )
        high = lax.ppermute(lax.slice_in_dim(block, 0, width, axis=dim), axis, backward)
        block = jnp.concatenate([low, block, high], axis=dim)
    return block


def signed_minmod(first, second):
    return 0.5 * (jnp.sign(first) + jnp.sign(second)) * jnp.minimum(jnp.abs(first), jnp.abs(second))


def trimmed(array, lower, upper, direction):
    return lax.slice_in_dim(array, lower, array.shape[direction] - upper, axis=direction)


def physical(state):
    mass_flux = state[0] * state[1]
    fluxes = jnp.stack(
        [
            mass_flux,
            mass_flux * state[1] + SOUND_SPEED * SOUND_SPEED * state[0],
            mass_flux * state[2],
        ]
    )
    conserved = jnp.stack([state[0], state[0] * state[1], state[0] * state[2]])
    return (fluxes, conserved)


def face_flux(left_state, right_state):
    left_flux, left_cons = physical(left_state)
    right_flux, right_cons = physical(right_state)
    signal = jnp.maximum(jnp.abs(left_state[1]), jnp.abs(right_state[1])) + SOUND_SPEED
    return 0.5 * (left_flux + right_flux) - 0.5 * signal * (right_cons - left_cons)


def primitive(conserved, normal):
    return jnp.stack(
        [conserved[0], conserved[normal] / conserved[0], conserved[3 - normal] / conserved[0]]
    )


def sweep_axis(prims, direction):
    slopes = signed_minmod(
        trimmed(prims, 1, 1, direction) - trimmed(prims, 0, 2, direction),
        trimmed(prims, 2, 0, direction) - trimmed(prims, 1, 1, direction),
    )
    left_state = trimmed(prims, 1, 2, direction) + 0.5 * trimmed(slopes, 0, 1, direction)
    right_state = trimmed(prims, 2, 1, direction) - 0.5 * trimmed(slopes, 1, 0, direction)
    fluxes = face_flux(left_state, right_state)
    return trimmed(fluxes, 1, 0, direction) - trimmed(fluxes, 0, 1, direction)


def strip_window(source, start, tile_width, fraction):
    window = lax.dynamic_slice_in_dim(source, start, tile_width + 1, source.ndim - 1)
    return (1.0 - fraction) * window[..., 1:] + fraction * window[..., :-1]


def row_barrel(rows, amounts, bit_count, sign):
    current = rows
    for level in range(bit_count):
        moved = jnp.roll(current, sign * 2**level, axis=2)
        taken = amounts // 2**level % 2 == 1
        current = jnp.where(taken[None, :, None], moved, current)
    return current


def sheared(strips, offset_cells, fraction):
    tile_width = strips.shape[3]
    total_cells = lax.axis_size("az") * tile_width
    backward = (total_cells - offset_cells - 1) % total_cells
    offsets = [offset_cells, backward]
    weights = [fraction, 1.0 - fraction]
    results = []
    offset_arr = jnp.stack(offsets)
    tiles = offset_arr // tile_width
    within = offset_arr % tile_width
    current = strips
    for level in range(lax.axis_size("az").bit_length() - 1):
        moved = passed_along(current, "az", 2**level)
        taken = tiles // 2**level % 2 == 1
        current = jnp.where(taken[:, None, None, None], moved, current)
    before = passed_along(current, "az", 1)
    joined = jnp.concatenate([before, current], axis=3)
    for side in range(2):
        start = tile_width - within[side] - 1
        results.append(strip_window(joined[side], start, tile_width, weights[side]))
    return jnp.stack(results)


def tendency(state, offset_cells, fraction, rotation):
    padded = padded_2(state, (("az", 2), ("rad", 1)), 2)
    columns = padded[:, :, 2:-2]
    strips = jnp.stack([columns[:, :2], columns[:, -2:]])
    ghosts = sheared(strips, offset_cells, fraction)
    radial = lax.axis_index("rad")
    lower_ghost = jnp.where(radial == 0, ghosts[0], columns[:, :2])
    upper_ghost = jnp.where(radial == lax.axis_size("rad") - 1, ghosts[1], columns[:, -2:])
    columns = jnp.concatenate([lower_ghost, columns[:, 2:-2], upper_ghost], axis=1)
    cycle_rows = padded[:, 2:-2, :]
    radial_div = sweep_axis(primitive(columns, 1), 1)
    azimuth_div = sweep_axis(primitive(cycle_rows, 2), 2)
    azimuth_div = jnp.stack([azimuth_div[0], azimuth_div[2], azimuth_div[1]])
    source = jnp.stack(
        [jnp.zeros_like(state[0]), 2.0 * rotation * state[2], -0.5 * rotation * state[1]]
    )
    return -(radial_div + azimuth_div) + source


def remap_rows(state, row_shift, row_frac):
    tile_width = state.shape[2]
    tiles = row_shift // tile_width
    within = row_shift % tile_width
    current = state
    for level in range(lax.axis_size("az").bit_length() - 1):
        moved = passed_along(current, "az", 2**level)
        taken = tiles // 2**level % 2 == 1
        current = jnp.where(taken[None, :, None], moved, current)
    before = passed_along(current, "az", 1)
    joined = jnp.concatenate([before, current], axis=2)
    lead = tile_width - within - 1
    aligned = row_barrel(joined, lead, tile_width.bit_length(), -1)
    weight = row_frac[None, :, None]
    return (1.0 - weight) * aligned[:, :, 1 : tile_width + 1] + weight * aligned[:, :, :tile_width]


def wide_ring(density, momentum, shear_shift, shear_frac, advect_shift, advect_frac, rotation):
    state = jnp.concatenate([density[None], momentum], axis=0)
    middle = state + TIME_STEP * tendency(state, shear_shift[0], shear_frac[0], rotation[0])
    final = 0.5 * state + 0.5 * (
        middle + TIME_STEP * tendency(middle, shear_shift[1], shear_frac[1], rotation[0])
    )
    remapped = remap_rows(final, advect_shift, advect_frac)
    return (remapped[0], remapped[1:])


def near(value):
    return pltpu.with_memory_space_constraint(value, pltpu.VMEM)


def per_device(density, momentum, shear_shift, shear_frac, advect_shift, advect_frac, rotation):
    tiles = lax.axis_size("az")
    radials = lax.axis_size("rad")
    rows, columns = density.shape
    sub = tiles * columns // LANES
    if tiles != 4 or sub != 8 or rows % 8 or radials % 2:
        return wide_ring(
            density, momentum, shear_shift, shear_frac, advect_shift, advect_frac, rotation
        )

    vmem = pl.BlockSpec(memory_space=pltpu.VMEM)
    smem = pl.BlockSpec(memory_space=pltpu.SMEM)

    def across(value, away):
        return lax.ppermute(value, "az", [(i, i ^ away) for i in range(tiles)])

    def swapped(value, lower):
        pairs = [((i + lower) % radials, (i + lower + 1) % radials) for i in range(0, radials, 2)]
        return lax.ppermute(value, "rad", pairs + [(b, a) for a, b in pairs])

    scalars = (shear_shift, shear_frac, advect_shift, advect_frac)
    spin = jnp.broadcast_to(rotation[:, None], (sub, LANES))
    edge, inner, weights, *kept = pl.pallas_call(
        split_kernel,
        out_shape=[
            pltpu.VMEM((3, 2 * HALO, columns), jnp.float32),
            pltpu.VMEM((3, rows - 2 * HALO, columns), jnp.float32),
            pltpu.VMEM((rows, LANES), jnp.float32),
        ]
        + [pltpu.SMEM(s.shape, s.dtype) for s in scalars[:3]],
        in_specs=[smem] * 4 + [vmem] * 2,
        out_specs=[vmem] * 3 + [smem] * 3,
    )(*scalars, density, momentum)
    edges = {0: edge}
    inners = {0: inner}
    for away in EDGE_ORDER:
        edges[away] = across(edge, away)
    for away in INNER_ORDER:
        inners[away] = across(inner, away)
    top = jnp.concatenate([edges[away][:, :HALO] for away in range(tiles)], axis=1)
    bottom = jnp.concatenate([edges[away][:, HALO:] for away in range(tiles)], axis=1)
    odd = lax.axis_index("rad") % 2 == 1
    between = swapped(jnp.where(odd, bottom, top), 1)
    within = swapped(jnp.where(odd, top, bottom), 0)
    operands = [edges[away] for away in (0,) + EDGE_ORDER]
    operands += [inners[away] for away in (0,) + INNER_ORDER]
    operands = [near(p) for p in [weights, spin] + operands + [within, between]]
    return pl.pallas_call(
        functools.partial(step_kernel, (tiles, radials, rows, columns, sub)),
        out_shape=[
            jax.ShapeDtypeStruct(density.shape, density.dtype),
            jax.ShapeDtypeStruct(momentum.shape, momentum.dtype),
        ],
        in_specs=[smem] * 3 + [vmem] * len(operands),
        out_specs=[vmem, vmem],
        scratch_shapes=[
            pltpu.VMEM((3, (rows + 17) * sub, LANES), jnp.float32),
            pltpu.VMEM((3, (rows + 4) * sub, LANES), jnp.float32),
            pltpu.VMEM((3, (rows + 1) * sub, LANES), jnp.float32),
        ]
        + [pltpu.VMEM((3, (rows + 16) * sub, LANES), jnp.float32)] * 4,
        compiler_params=pltpu.CompilerParams(vmem_limit_bytes=40 * 2**20),
    )(*kept, *operands)


def solution(mesh):
    in_specs = (
        P(("groups", "rad"), "az"),
        P("groups", "rad", "az"),
        P("groups"),
        P("groups"),
        P(("groups", "rad")),
        P(("groups", "rad")),
        P("groups"),
    )
    out_specs = (P(("groups", "rad"), "az"), P("groups", "rad", "az"))
    return jax.shard_map(
        per_device, mesh=mesh, in_specs=in_specs, out_specs=out_specs, check_vma=False
    )
```

```python
import functools

import jax
import jax.numpy as jnp
from jax import lax
from jax.experimental import pallas as pl
from jax.experimental.pallas import tpu as pltpu
from jax.sharding import PartitionSpec as P

TIME_STEP = 0.12
SOUND_SPEED = 1.0
LANES = 128
HALO = 4
EDGE_ORDER = (1, 3, 2)
INNER_ORDER = (2, 1, 3)
LOOPS = (1, 1, 2)


def turned(value, whole, part, lane):
    lanes = pltpu.roll(value, part, 1)
    same = pltpu.roll(lanes, whole, 0)
    before = pltpu.roll(same, 1, 0)
    return jnp.where(lane < part, before, same)


def previous(value, lane):
    lanes = pltpu.roll(value, 1, 1)
    return jnp.where(lane == 0, pltpu.roll(lanes, 1, 0), lanes)


def following(value, lane):
    lanes = pltpu.roll(value, LANES - 1, 1)
    return jnp.where(lane == LANES - 1, pltpu.roll(lanes, value.shape[0] - 1, 0), lanes)


def minmod(first, second):
    return jnp.maximum(jnp.minimum(second, 0.0), jnp.minimum(first, jnp.maximum(second, 0.0)))


def sums(left, right):
    signal = jnp.maximum(jnp.abs(left[1]), jnp.abs(right[1])) + 1.0
    lower = left[0] * (left[1] + signal)
    upper = right[0] * (right[1] - signal)
    return (
        lower + upper,
        (left[1] * lower + left[0]) + (right[1] * upper + right[0]),
        left[2] * lower + right[2] * upper,
    )


def minus(first, second):
    return tuple(a - b for a, b in zip(first, second))


def plus(first, second):
    return tuple(a + b for a, b in zip(first, second))


def primitives(state):
    inverse = 1.0 / state[0]
    return state[0], state[1] * inverse, state[2] * inverse


def azimuthal(whole):
    return whole[0], whole[2], whole[1]


def repeated(first, count, loops, body):
    each = count // loops

    def block(turn, carry):
        for step in range(each):
            body(first + turn * each + step)
        return carry

    if loops == 1:
        block(0, 0)
    else:
        lax.fori_loop(0, loops, block, 0)


def radial_sweep(load, emit, first, count, loops):
    def half_steps(above, below):
        return tuple(0.5 * (a - b) for a, b in zip(above, below))

    def advance(row, carry):
        whole = load(row)
        ahead = half_steps(whole, carry["whole"])
        slope = tuple(minmod(b, a) for b, a in zip(carry["ahead"], ahead))
        face = sums(carry["left"], minus(carry["whole"], slope))
        new = {"whole": whole, "ahead": ahead, "left": plus(carry["whole"], slope), "face": face}
        return new, minus(face, carry["face"])

    rows = [load(first - 2 + k) for k in range(4)]
    ahead = [half_steps(rows[k + 1], rows[k]) for k in range(3)]
    slopes = [tuple(minmod(b, a) for b, a in zip(ahead[k], ahead[k + 1])) for k in range(2)]
    carry = {
        "whole": rows[3],
        "ahead": ahead[2],
        "left": plus(rows[2], slopes[1]),
        "face": sums(plus(rows[1], slopes[0]), minus(rows[2], slopes[1])),
    }
    each = count // loops

    def block(turn, carry):
        for step in range(each):
            row = first + turn * each + step
            carry, across = advance(row + 2, carry)
            emit(row, across)
        return carry

    if loops == 1:
        block(0, carry)
    else:
        lax.fori_loop(0, loops, block, carry)


def split_kernel(*refs):
    advect_frac, density, momentum, edges, inner, weights = refs[3:9]
    for given, kept in zip(refs[:3], refs[9:]):
        for place in range(given.shape[0]):
            kept[place] = given[place]
    rows = density.shape[0]
    for component, take in enumerate(
        (lambda cut: density[cut, :], lambda cut: momentum[0, cut, :], lambda cut: momentum[1, cut, :])
    ):
        edges[component, 0:HALO] = take(slice(0, HALO))
        edges[component, HALO : 2 * HALO] = take(slice(rows - HALO, rows))
        inner[component] = take(slice(HALO, rows - HALO))
    for row in range(rows):
        weights[row : row + 1, :] = jnp.full((1, LANES), advect_frac[row], jnp.float32)


def step_kernel(sizes, *refs):
    tiles, radials, rows, columns, sub = sizes
    per_tile = columns // LANES
    shear_shift, shear_frac, advect_shift, weights, rotation = refs[:5]
    inners = dict(zip((0,) + INNER_ORDER, refs[5 : 5 + tiles]))
    edges = dict(zip((0,) + EDGE_ORDER, refs[5 + tiles : 5 + 2 * tiles]))
    within, between, density_out, momentum_out, start, middle, remapped, whole, lower, upper, faces = refs[5 + 2 * tiles :]
    lane = lax.broadcasted_iota(jnp.int32, (sub, LANES), 1)
    az = lax.axis_index("az")
    radial = lax.axis_index("rad")
    main = 6
    end = main + rows + 4
    odd = radial % 2
    spot_within = jnp.where(odd == 1, 0, end + 2)
    spot_between = jnp.where(odd == 1, end + 2, 0)

    def place(value, component, row, tile, part):
        first = row * sub + tile * per_tile + part
        start[component, pl.ds(first, value.shape[0], stride=sub), :] = value

    for away in range(tiles):
        tile = az ^ away
        for part in range(per_tile):
            cut = slice(part * LANES, (part + 1) * LANES)
            for component in range(3):
                place(edges[away][component, 0:HALO, cut], component, main + 2, tile, part)
                place(edges[away][component, HALO : 2 * HALO, cut], component, end - 2 - HALO, tile, part)
                for row in range(0, rows - 2 * HALO, 8):
                    place(inners[away][component, row : row + 8, cut], component, main + 2 + HALO + row, tile, part)
                border = slice(HALO * away, HALO * away + HALO)
                place(within[component, border, cut], component, spot_within, tile, part)
                place(between[component, border, cut], component, spot_between, tile, part)

    def row_of(ref, component, row):
        return ref[component, pl.ds(row * sub if isinstance(row, int) else pl.multiple_of(row * sub, 8), sub), :]

    def state_of(ref, row):
        return tuple(row_of(ref, component, row) for component in range(3))

    def put(ref, row, state):
        for component in range(3):
            ref[component, pl.ds(row * sub if isinstance(row, int) else pl.multiple_of(row * sub, 8), sub), :] = state[component]

    at_low = radial == 0
    at_high = radial == radials - 1
    total = sub * LANES

    def from_below(state, section, here):
        shift = jnp.where(here, shear_shift[section], 0)
        weight = jnp.where(here, shear_frac[section], 0.0)
        moved = tuple(turned(s, shift // LANES, shift % LANES, lane) for s in state)
        return tuple((1.0 - weight) * m + weight * previous(m, lane) for m in moved)

    def from_above(state, section, here):
        shift = jnp.where(here, (total - shear_shift[section]) % total, 0)
        weight = jnp.where(here, shear_frac[section], 0.0)
        moved = tuple(turned(s, shift // LANES, shift % LANES, lane) for s in state)
        return tuple((1.0 - weight) * m + weight * following(m, lane) for m in moved)

    for k in range(2):
        put(start, main + k, from_below(state_of(start, 2 + k), 0, at_low))
        put(start, end - 2 + k, from_above(state_of(start, end + 2 + k), 0, at_high))
        put(start, 4 + k, from_above(state_of(start, main + 2 + k), 0, at_low))
        put(start, end + k, from_below(state_of(start, end - 4 + k), 0, at_high))

    spin = rotation[...]

    def changed(state, double):
        half_step = 0.5 * TIME_STEP
        return (
            state[0] - half_step * double[0],
            state[1] - half_step * double[1] + (2.0 * TIME_STEP) * spin * state[2],
            state[2] - half_step * double[2] - (0.5 * TIME_STEP) * spin * state[1],
        )

    def slopes(source, row):
        values = primitives(state_of(source, row))
        put(whole, row, values)
        normal = azimuthal(values)
        halves = tuple(0.5 * n for n in normal)
        slope = tuple(
            minmod(h - previous(h, lane), following(h, lane) - h) for h in halves
        )
        put(lower, row, plus(normal, slope))
        put(upper, row, minus(normal, slope))

    def meet(row):
        right = tuple(following(r, lane) for r in state_of(upper, row))
        put(faces, row, sums(state_of(lower, row), right))

    def turn(row):
        face = state_of(faces, row)
        return azimuthal(minus(face, tuple(previous(f, lane) for f in face)))

    def only(source, row):
        put(whole, row, primitives(state_of(source, row)))

    def emit_first(shift):
        def emit(row, across):
            put(middle, row + shift, changed(state_of(start, row), plus(across, turn(row))))
        return emit

    for row in (0, 1, 4, 5, main, main + 1, end - 2, end - 1, end, end + 1, end + 4, end + 5):
        only(start, row)
    for row in (2, 3, end + 2, end + 3):
        slopes(start, row)
    repeated(main + 2, rows, LOOPS[0], lambda row: slopes(start, row))
    for row in (2, 3, end + 2, end + 3):
        meet(row)
    repeated(main + 2, rows, LOOPS[1], meet)
    radial_sweep(lambda row: state_of(whole, row), emit_first(-2), 2, 2, 1)
    radial_sweep(lambda row: state_of(whole, row), emit_first(rows - end), end + 2, 2, 1)
    radial_sweep(lambda row: state_of(whole, row), emit_first(-main), main + 2, rows, LOOPS[2])

    for k in range(2):
        put(middle, k, from_below(state_of(middle, k), 1, at_low))
        put(middle, rows + 2 + k, from_above(state_of(middle, rows + 2 + k), 1, at_high))

    def emit_second(row, across):
        new = changed(state_of(middle, row), plus(across, turn(row)))
        old = state_of(start, row + main)
        final = tuple(0.5 * (o + n) for o, n in zip(old, new))
        shift = advect_shift[row - 2]
        put(remapped, row - 2, tuple(turned(f, shift // LANES, shift % LANES, lane) for f in final))

    for row in (0, 1, rows + 2, rows + 3):
        only(middle, row)
    repeated(2, rows, LOOPS[0], lambda row: slopes(middle, row))
    repeated(2, rows, LOOPS[1], meet)
    radial_sweep(lambda row: state_of(whole, row), emit_second, 2, rows, LOOPS[2])

    for row in range(0, rows, 8):
        weight = weights[row : row + 8, :]
        for component in range(3):
            spots = [(az * per_tile + part + sub - 1) % sub for part in range(per_tile + 1)]
            tiles_here = [remapped[component, pl.ds(row * sub + spot, 8, stride=sub), :] for spot in spots]
            moved = [pltpu.roll(t, 1, 1) for t in tiles_here]
            for part in range(per_tile):
                cut = slice(part * LANES, (part + 1) * LANES)
                before = jnp.where(lane == 0, moved[part], moved[part + 1])
                value = (1.0 - weight) * tiles_here[part + 1] + weight * before
                if component == 0:
                    density_out[row : row + 8, cut] = value
                else:
                    momentum_out[component - 1, row : row + 8, cut] = value


def passed_along(value, axis, steps):
    count = lax.axis_size(axis)
    pairs = [(source, (source + steps) % count) for source in range(count)]
    return lax.ppermute(value, axis, pairs)


def padded_2(block, sides, width):
    for axis, dim in sides:
        count = lax.axis_size(axis)
        forward = [(i, i + 1) for i in range(count - 1)]
        forward.append((count - 1, 0))
        backward = [(target, source) for source, target in forward]
        low = lax.ppermute(
            lax.slice_in_dim(block, block.shape[dim] - width, None, axis=dim), axis, forward
        )
        high = lax.ppermute(lax.slice_in_dim(block, 0, width, axis=dim), axis, backward)
        block = jnp.concatenate([low, block, high], axis=dim)
    return block


def signed_minmod(first, second):
    return 0.5 * (jnp.sign(first) + jnp.sign(second)) * jnp.minimum(jnp.abs(first), jnp.abs(second))


def trimmed(array, lower, upper, direction):
    return lax.slice_in_dim(array, lower, array.shape[direction] - upper, axis=direction)


def physical(state):
    mass_flux = state[0] * state[1]
    fluxes = jnp.stack(
        [
            mass_flux,
            mass_flux * state[1] + SOUND_SPEED * SOUND_SPEED * state[0],
            mass_flux * state[2],
        ]
    )
    conserved = jnp.stack([state[0], state[0] * state[1], state[0] * state[2]])
    return (fluxes, conserved)


def face_flux(left_state, right_state):
    left_flux, left_cons = physical(left_state)
    right_flux, right_cons = physical(right_state)
    signal = jnp.maximum(jnp.abs(left_state[1]), jnp.abs(right_state[1])) + SOUND_SPEED
    return 0.5 * (left_flux + right_flux) - 0.5 * signal * (right_cons - left_cons)


def primitive(conserved, normal):
    return jnp.stack(
        [conserved[0], conserved[normal] / conserved[0], conserved[3 - normal] / conserved[0]]
    )


def sweep_axis(prims, direction):
    slopes = signed_minmod(
        trimmed(prims, 1, 1, direction) - trimmed(prims, 0, 2, direction),
        trimmed(prims, 2, 0, direction) - trimmed(prims, 1, 1, direction),
    )
    left_state = trimmed(prims, 1, 2, direction) + 0.5 * trimmed(slopes, 0, 1, direction)
    right_state = trimmed(prims, 2, 1, direction) - 0.5 * trimmed(slopes, 1, 0, direction)
    fluxes = face_flux(left_state, right_state)
    return trimmed(fluxes, 1, 0, direction) - trimmed(fluxes, 0, 1, direction)


def strip_window(source, start, tile_width, fraction):
    window = lax.dynamic_slice_in_dim(source, start, tile_width + 1, source.ndim - 1)
    return (1.0 - fraction) * window[..., 1:] + fraction * window[..., :-1]


def row_barrel(rows, amounts, bit_count, sign):
    current = rows
    for level in range(bit_count):
        moved = jnp.roll(current, sign * 2**level, axis=2)
        taken = amounts // 2**level % 2 == 1
        current = jnp.where(taken[None, :, None], moved, current)
    return current


def sheared(strips, offset_cells, fraction):
    tile_width = strips.shape[3]
    total_cells = lax.axis_size("az") * tile_width
    backward = (total_cells - offset_cells - 1) % total_cells
    offsets = [offset_cells, backward]
    weights = [fraction, 1.0 - fraction]
    results = []
    offset_arr = jnp.stack(offsets)
    tiles = offset_arr // tile_width
    within = offset_arr % tile_width
    current = strips
    for level in range(lax.axis_size("az").bit_length() - 1):
        moved = passed_along(current, "az", 2**level)
        taken = tiles // 2**level % 2 == 1
        current = jnp.where(taken[:, None, None, None], moved, current)
    before = passed_along(current, "az", 1)
    joined = jnp.concatenate([before, current], axis=3)
    for side in range(2):
        start = tile_width - within[side] - 1
        results.append(strip_window(joined[side], start, tile_width, weights[side]))
    return jnp.stack(results)


def tendency(state, offset_cells, fraction, rotation):
    padded = padded_2(state, (("az", 2), ("rad", 1)), 2)
    columns = padded[:, :, 2:-2]
    strips = jnp.stack([columns[:, :2], columns[:, -2:]])
    ghosts = sheared(strips, offset_cells, fraction)
    radial = lax.axis_index("rad")
    lower_ghost = jnp.where(radial == 0, ghosts[0], columns[:, :2])
    upper_ghost = jnp.where(radial == lax.axis_size("rad") - 1, ghosts[1], columns[:, -2:])
    columns = jnp.concatenate([lower_ghost, columns[:, 2:-2], upper_ghost], axis=1)
    cycle_rows = padded[:, 2:-2, :]
    radial_div = sweep_axis(primitive(columns, 1), 1)
    azimuth_div = sweep_axis(primitive(cycle_rows, 2), 2)
    azimuth_div = jnp.stack([azimuth_div[0], azimuth_div[2], azimuth_div[1]])
    source = jnp.stack(
        [jnp.zeros_like(state[0]), 2.0 * rotation * state[2], -0.5 * rotation * state[1]]
    )
    return -(radial_div + azimuth_div) + source


def remap_rows(state, row_shift, row_frac):
    tile_width = state.shape[2]
    tiles = row_shift // tile_width
    within = row_shift % tile_width
    current = state
    for level in range(lax.axis_size("az").bit_length() - 1):
        moved = passed_along(current, "az", 2**level)
        taken = tiles // 2**level % 2 == 1
        current = jnp.where(taken[None, :, None], moved, current)
    before = passed_along(current, "az", 1)
    joined = jnp.concatenate([before, current], axis=2)
    lead = tile_width - within - 1
    aligned = row_barrel(joined, lead, tile_width.bit_length(), -1)
    weight = row_frac[None, :, None]
    return (1.0 - weight) * aligned[:, :, 1 : tile_width + 1] + weight * aligned[:, :, :tile_width]


def wide_ring(density, momentum, shear_shift, shear_frac, advect_shift, advect_frac, rotation):
    state = jnp.concatenate([density[None], momentum], axis=0)
    middle = state + TIME_STEP * tendency(state, shear_shift[0], shear_frac[0], rotation[0])
    final = 0.5 * state + 0.5 * (
        middle + TIME_STEP * tendency(middle, shear_shift[1], shear_frac[1], rotation[0])
    )
    remapped = remap_rows(final, advect_shift, advect_frac)
    return (remapped[0], remapped[1:])


def near(value):
    return pltpu.with_memory_space_constraint(value, pltpu.VMEM)


def per_device(density, momentum, shear_shift, shear_frac, advect_shift, advect_frac, rotation):
    tiles = lax.axis_size("az")
    radials = lax.axis_size("rad")
    rows, columns = density.shape
    sub = tiles * columns // LANES
    if tiles != 4 or sub != 8 or rows % 8 or radials % 2:
        return wide_ring(
            density, momentum, shear_shift, shear_frac, advect_shift, advect_frac, rotation
        )

    vmem = pl.BlockSpec(memory_space=pltpu.VMEM)
    smem = pl.BlockSpec(memory_space=pltpu.SMEM)

    def across(value, away):
        return lax.ppermute(value, "az", [(i, i ^ away) for i in range(tiles)])

    def swapped(value, lower):
        pairs = [((i + lower) % radials, (i + lower + 1) % radials) for i in range(0, radials, 2)]
        return lax.ppermute(value, "rad", pairs + [(b, a) for a, b in pairs])

    scalars = (shear_shift, shear_frac, advect_shift, advect_frac)
    spin = jnp.broadcast_to(rotation[:, None], (sub, LANES))
    edge, inner, weights, *kept = pl.pallas_call(
        split_kernel,
        out_shape=[
            pltpu.VMEM((3, 2 * HALO, columns), jnp.float32),
            pltpu.VMEM((3, rows - 2 * HALO, columns), jnp.float32),
            pltpu.VMEM((rows, LANES), jnp.float32),
        ]
        + [pltpu.SMEM(s.shape, s.dtype) for s in scalars[:3]],
        in_specs=[smem] * 4 + [vmem] * 2,
        out_specs=[vmem] * 3 + [smem] * 3,
    )(*scalars, density, momentum)
    edges = {0: edge}
    inners = {0: inner}
    for away in EDGE_ORDER:
        edges[away] = across(edge, away)
    for away in INNER_ORDER:
        inners[away] = across(inner, away)
    top = jnp.concatenate([edges[away][:, :HALO] for away in range(tiles)], axis=1)
    bottom = jnp.concatenate([edges[away][:, HALO:] for away in range(tiles)], axis=1)
    odd = lax.axis_index("rad") % 2 == 1
    between = swapped(jnp.where(odd, bottom, top), 1)
    within = swapped(jnp.where(odd, top, bottom), 0)
    operands = [inners[away] for away in (0,) + INNER_ORDER]
    operands += [edges[away] for away in (0,) + EDGE_ORDER]
    operands = [near(p) for p in [weights, spin] + operands + [within, between]]
    return pl.pallas_call(
        functools.partial(step_kernel, (tiles, radials, rows, columns, sub)),
        out_shape=[
            jax.ShapeDtypeStruct(density.shape, density.dtype),
            jax.ShapeDtypeStruct(momentum.shape, momentum.dtype),
        ],
        in_specs=[smem] * 3 + [vmem] * len(operands),
        out_specs=[vmem, vmem],
        scratch_shapes=[
            pltpu.VMEM((3, (rows + 17) * sub, LANES), jnp.float32),
            pltpu.VMEM((3, (rows + 4) * sub, LANES), jnp.float32),
            pltpu.VMEM((3, (rows + 1) * sub, LANES), jnp.float32),
        ]
        + [pltpu.VMEM((3, (rows + 16) * sub, LANES), jnp.float32)] * 4,
        compiler_params=pltpu.CompilerParams(vmem_limit_bytes=40 * 2**20),
    )(*kept, *operands)


def solution(mesh):
    in_specs = (
        P(("groups", "rad"), "az"),
        P("groups", "rad", "az"),
        P("groups"),
        P("groups"),
        P(("groups", "rad")),
        P(("groups", "rad")),
        P("groups"),
    )
    out_specs = (P(("groups", "rad"), "az"), P("groups", "rad", "az"))
    return jax.shard_map(
        per_device, mesh=mesh, in_specs=in_specs, out_specs=out_specs, check_vma=False
    )
```
